512 devices in a mesh: row: 16 (over x, z_hi), col: 16 (over y, z_lo), layer: 2 (over core).
Axes of the slice: x: 4, y: 8, z: 8 (z_hi: 4, z_lo: 2; z = z_hi * 2 + z_lo), core: 2. Of those that a mesh axis runs over, the one named last changes fastest.
Arguments:
- matrix: float32 [8192, 8192], P('row', 'col'), may hold values from -1 to 1
- band_cols: int32 [64, 17], replicated, may hold values from 0 to 63, as said below
Outputs:
- new_sign: float32 [8192, 8192], P('row', ('col', 'layer'))
- square: float32 [8192, 8192], P('row', ('col', 'layer'))
The draws below stay inside these ranges and needn't reach their ends.
Inputs may be any that keep to these rules, and one draw needn't show every extreme that they name: `band_cols`: row p lists 17 different block columns, p itself among them, each q with |q - p| <= 16; the band does not wrap around.
All inputs are finite; a program needn't handle non-finite values.
Results may differ from the reference program's by a relative error of at most 0.0048.
Values may be sent and summed in bfloat16 or wider, within the bound.
A program may use at most 64 MiB of HBM per device.

```python
import math
import jax
import jax.numpy as jnp

BLOCK = 128
NB = 64
HB = 16
K = 17


def draw_matrix(key, part):
    key = jax.random.fold_in(key, 1)
    first_key, second_key, third_key = jax.random.split(key, 3)
    total = NB * BLOCK
    spread = 0.5 / math.sqrt(K * BLOCK)
    noise = jax.random.normal(first_key, (total, total), jnp.float32) * spread
    magnitude = jax.random.uniform(second_key, (total,), jnp.float32, 0.3, 0.8)
    signs = jnp.where(jax.random.randint(third_key, (total,), 0, 2) == 1, 1.0, -1.0)
    places = jnp.arange(total, dtype=jnp.int32)
    diagonal = places[:, None] == places[None, :]
    return (noise + jnp.where(diagonal, (magnitude * signs)[:, None], 0.0)).astype(jnp.float32)


def draw_band_cols(key, part):
    key = jax.random.fold_in(key, 2)
    slots = jnp.arange(2 * HB, dtype=jnp.int32)
    offsets_all = jnp.where(slots < HB, slots - HB, slots - HB + 1)
    rows = jnp.arange(NB, dtype=jnp.int32)[:, None]
    targets = rows + offsets_all[None, :]
    outside = ((targets < 0) | (targets >= NB)).astype(jnp.int32)
    scores = jax.random.randint(key, (NB, 2 * HB), 0, 1 << 20) * (2 * HB) + slots[None, :] + outside * (1 << 28)
    order = jnp.argsort(scores, axis=1, stable=True).astype(jnp.int32)
    chosen = order[:, :K - 1]
    offsets = jnp.where(chosen < HB, chosen - HB, chosen - HB + 1)
    columns = rows + offsets
    return jnp.concatenate([rows, columns], axis=1).astype(jnp.int32)


def setup_inputs(seed: int = 0) -> dict:
    keys = jax.random.split(jax.random.key(seed), 3)
    matrix = draw_matrix(jax.random.fold_in(keys[2], 71), 0)
    band_cols = draw_band_cols(jax.random.fold_in(keys[2], 71), 0)
    return {"matrix": matrix, "band_cols": band_cols}


def reference(matrix, band_cols):
    nblocks = band_cols.shape[0]
    size = matrix.shape[0] // nblocks
    pattern = jnp.any(band_cols[:, :, None] == jnp.arange(nblocks, dtype=jnp.int32)[None, None, :], axis=1).astype(jnp.float32)
    mask = jnp.broadcast_to(pattern[:, None, :, None], (nblocks, size, nblocks, size)).reshape(matrix.shape)
    sparse = mask * matrix
    lower = sparse.astype(jnp.bfloat16)
    square = mask * jnp.dot(lower, lower, preferred_element_type=jnp.float32)
    square_low = square.astype(jnp.bfloat16)
    cubes = jnp.dot(lower, square_low, preferred_element_type=jnp.float32)
    new_sign = mask * (1.5 * sparse - 0.5 * cubes)
    return new_sign, square
```

```python
import jax
import jax.numpy as jnp
from jax import lax
from jax.experimental import pallas as pl
from jax.experimental.pallas import tpu as pltpu
from jax.sharding import PartitionSpec as P

BLOCK = 128
REACH = 4
PIECES = 4
MESH = pl.DeviceIdType.MESH


def kernel(band_ref, mat_ref, sign_ref, square_ref, left, right, cube, mask_ref, acc,
           left_recv, sib_recv, right_recv, cube_recv, send_sems):
    r = lax.axis_index("row")
    c = lax.axis_index("col")
    l = lax.axis_index("layer")
    tile = mat_ref.shape[0]
    width = tile // 2
    count = tile // BLOCK
    piece = tile // PIECES
    x, zh = r // 4, r % 4
    y, zl = c // 2, c % 2
    ol = 1 - zl

    def at(dx=0, dzh=0, dy=0, zlow=None):
        zlow = zl if zlow is None else zlow
        return (((x + dx + 4) % 4) * 4 + (zh + dzh + 4) % 4, ((y + dy + 8) % 8) * 2 + zlow, l)

    up, down = at(dy=1), at(dy=-1)
    pair = at(zlow=ol)
    zup, zdown = at(dzh=1), at(dzh=-1)
    xup, xdown = at(dx=1), at(dx=-1)
    sibling = (r, c, 1 - l)

    barrier = pltpu.get_barrier_semaphore()
    for other in (up, down, pair, zup, zdown, xup, xdown, sibling):
        pl.semaphore_signal(barrier, inc=1, device_id=other, device_id_type=MESH)

    column = 4 * c + lax.broadcasted_iota(jnp.int32, (1, tile), 1) // BLOCK
    own_left = 4 + zl
    own_right = 4 + zh
    for a in range(count):
        hit = column == band_ref[count * r + a, 0]
        for j in range(1, band_ref.shape[1]):
            hit = hit | (column == band_ref[count * r + a, j])
        row_mask = jnp.where(hit, 1.0, 0.0).astype(jnp.float32)
        mask_ref[pl.ds(a, 1), :] = row_mask
        rows = pl.ds(a * BLOCK, BLOCK)
        low = (mat_ref[rows, :] * row_mask).astype(jnp.bfloat16)
        left[own_left, 0, rows, :] = low[:, :width]
        left[own_left, 1, rows, :] = low[:, width:]
        right[own_right, rows, :] = left[own_left, l, rows, :]

    pl.semaphore_wait(barrier, 8)

    sent = []

    def send(src, dst, recv_sem, device):
        copy = pltpu.make_async_remote_copy(
            src_ref=src, dst_ref=dst, send_sem=send_sems.at[len(sent)], recv_sem=recv_sem,
            device_id=device, device_id_type=MESH)
        copy.start()
        sent.append(copy)

    def arrived(ref, sem):
        pltpu.make_async_remote_copy(
            src_ref=ref, dst_ref=ref, send_sem=send_sems.at[0], recv_sem=sem,
            device_id=sibling, device_id_type=MESH).wait_recv()

    def part(p):
        return pl.ds(p * piece, piece)

    def send_left(slot, to_slot, p, device):
        send(left.at[slot, l, part(p)], left.at[to_slot, l, part(p)], left_recv.at[to_slot, p], device)

    def wait_left(slot, p):
        arrived(left.at[slot, l, part(p)], left_recv.at[slot, p])
        send(left.at[slot, l, part(p)], left.at[slot, l, part(p)], sib_recv.at[slot, p], sibling)

    def column_start(buf, sem, p):
        src = buf.at[own_right, part(p)]
        send(src, src, sem.at[own_right, p], zup)
        send(src, src, sem.at[own_right, p], zdown)
        send(src, buf.at[zh, part(p)], sem.at[zh, p], xup)
        send(src, buf.at[8 + zh, part(p)], sem.at[8 + zh, p], xdown)

    def along_x(buf, sem, zs, p):
        higher = zs > zh
        slot = jnp.where(higher, zs, 8 + zs)
        device = (jnp.where(higher, xup[0], xdown[0]), c, l)
        send(buf.at[4 + zs, part(p)], buf.at[slot, part(p)], sem.at[slot, p], device)

    def column_near(buf, sem, p):
        for step in (-1, 1):
            zs = (zh + step + 4) % 4
            slot = 4 + zs
            arrived(buf.at[slot, part(p)], sem.at[slot, p])
            if (p < PIECES // 2) == (step == -1):
                send(buf.at[slot, part(p)], buf.at[slot, part(p)], sem.at[slot, p], zup if step == -1 else zdown)
            along_x(buf, sem, zs, p)

    def column_far(buf, sem, p):
        zs = (zh + 2) % 4
        arrived(buf.at[4 + zs, part(p)], sem.at[4 + zs, p])
        along_x(buf, sem, zs, p)

    def column_end(buf, sem):
        for p in range(PIECES):
            arrived(buf.at[zh, part(p)], sem.at[zh, p])
            arrived(buf.at[8 + zh, part(p)], sem.at[8 + zh, p])
            for step in (1, 3, 2):
                zs = (zh + step) % 4
                slot = jnp.where(zs > zh, zs, 8 + zs)
                arrived(buf.at[slot, part(p)], sem.at[slot, p])

    far_src = jnp.where(zl == 0, 3, 6)
    far_dst = jnp.where(zl == 0, 1, 8)
    far_device = (r, jnp.where(zl == 0, up[1], down[1]), l)

    for p in range(PIECES):
        column_start(right, right_recv, p)
        send_left(own_left, 2 + zl, p, up)
        send_left(own_left, 6 + zl, p, down)
        send_left(own_left, own_left, p, pair)
    for p in range(PIECES):
        wait_left(2 + zl, p)
        send_left(2 + zl, zl, p, up)
        wait_left(6 + zl, p)
        send_left(6 + zl, 8 + zl, p, down)
        wait_left(4 + ol, p)
        send_left(4 + ol, 2 + ol, p, up)
        send_left(4 + ol, 6 + ol, p, down)
        column_near(right, right_recv, p)
    for p in range(PIECES):
        wait_left(2 + ol, p)
        wait_left(6 + ol, p)
        send_left(far_src, far_dst, p, far_device)
        column_far(right, right_recv, p)
    for p in range(PIECES):
        wait_left(zl, p)
        wait_left(8 + zl, p)
        wait_left(far_dst, p)
    for p in range(PIECES):
        for slot in (2 + zl, 6 + zl, 4 + ol, 2 + ol, 6 + ol, zl, 8 + zl, far_dst):
            arrived(left.at[slot, 1 - l, part(p)], sib_recv.at[slot, p])
    column_end(right, right_recv)

    first = jnp.maximum(jnp.maximum(r, c) - REACH, 0)
    last = jnp.minimum(jnp.minimum(r, c) + REACH, 15)
    inside = (c - r <= REACH) & (r - c <= REACH)
    stop = jnp.where(inside, last + 1, first)

    def product(buf):
        acc[...] = jnp.zeros_like(acc)

        def body(k, carry):
            ls = k - c + zl + 4
            rs = k - r + zh + 4
            acc[...] += jnp.dot(left[ls, 0], buf[rs, :width, :], preferred_element_type=jnp.float32) + jnp.dot(
                left[ls, 1], buf[rs, width:, :], preferred_element_type=jnp.float32)
            return carry

        lax.fori_loop(first, stop, body, 0)

    half = pl.ds(pl.multiple_of(l * width, width), width)
    product(right)
    for a in range(count):
        rows = pl.ds(a * BLOCK, BLOCK)
        value = acc[rows, :] * mask_ref[pl.ds(a, 1), half]
        square_ref[rows, :] = value
        cube[own_right, rows, :] = value.astype(jnp.bfloat16)

    for p in range(PIECES):
        column_start(cube, cube_recv, p)
    for p in range(PIECES):
        column_near(cube, cube_recv, p)
    for p in range(PIECES):
        column_far(cube, cube_recv, p)
    column_end(cube, cube_recv)

    product(cube)
    for a in range(count):
        rows = pl.ds(a * BLOCK, BLOCK)
        row_mask = mask_ref[pl.ds(a, 1), half]
        sparse = mat_ref[rows, half] * row_mask
        sign_ref[rows, :] = row_mask * (1.5 * sparse - 0.5 * acc[rows, :])

    for copy in sent:
        copy.wait_send()


def per_device(matrix, band_cols):
    tile = matrix.shape[0]
    width = tile // 2
    out = jax.ShapeDtypeStruct((tile, width), jnp.float32)
    return pl.pallas_call(
        kernel,
        out_shape=(out, out),
        in_specs=[pl.BlockSpec(memory_space=pltpu.SMEM), pl.BlockSpec(memory_space=pltpu.VMEM)],
        out_specs=(pl.BlockSpec(memory_space=pltpu.VMEM),) * 2,
        scratch_shapes=[
            pltpu.VMEM((10, 2, tile, width), jnp.bfloat16),
            pltpu.VMEM((12, tile, width), jnp.bfloat16),
            pltpu.VMEM((12, tile, width), jnp.bfloat16),
            pltpu.VMEM((8, tile), jnp.float32),
            pltpu.VMEM((tile, width), jnp.float32),
            pltpu.SemaphoreType.DMA((10, PIECES)),
            pltpu.SemaphoreType.DMA((10, PIECES)),
            pltpu.SemaphoreType.DMA((12, PIECES)),
            pltpu.SemaphoreType.DMA((12, PIECES)),
            pltpu.SemaphoreType.DMA((32 * PIECES,)),
        ],
        compiler_params=pltpu.CompilerParams(
            collective_id=0, has_side_effects=True, vmem_limit_bytes=48 * 2**20),
        cost_estimate=pl.CostEstimate(flops=4 * 10**9, bytes_accessed=2 * 2**20, transcendentals=0),
    )(band_cols, matrix)


def solution(mesh):
    in_specs = (P("row", "col"), P())
    out_specs = (P("row", ("col", "layer")), P("row", ("col", "layer")))
    return jax.shard_map(
        per_device, mesh=mesh, in_specs=in_specs, out_specs=out_specs, check_vma=False
    )
```

```python
import jax
import jax.numpy as jnp
from jax import lax
from jax.experimental import pallas as pl
from jax.experimental.pallas import tpu as pltpu
from jax.sharding import PartitionSpec as P

BLOCK = 128
REACH = 4
PIECES = 4
MESH = pl.DeviceIdType.MESH
EVERY, FRONT, HALVES = (0, 1, 2, 3), (0, 1), (0, 1)
COLUMN = [
    ("A1", "zp", None, EVERY), ("B1", "zo", None, EVERY), ("A2", "zo", "A1", EVERY), ("B2", "zp", "B1", EVERY),
    ("A3", "zp", "A2", FRONT), ("B3", "zo", "B2", FRONT), ("A4", "zo", "A3", FRONT), ("B4", "zp", "B3", FRONT),
    ("XO", "x", None, EVERY), ("XS", "w", None, HALVES), ("XA", "x", "A2", EVERY), ("XB", "x", "B2", EVERY),
    ("KA", "w", "XA", (0,)), ("KB", "w", "XB", (0,)), ("LA", "w", "KA", (0,)), ("LB", "w", "KB", (0,)),
    ("FA", "x", "A4", FRONT), ("FB", "x", "B4", FRONT),
]
ROW = [
    ("YF", "yf", None, HALVES), ("YN", "yn", None, HALVES), ("TF", "yf", "YF", HALVES), ("TN", "yn", "YN", HALVES),
    ("PF", "yf", "A1", HALVES), ("PN", "yn", "A1", HALVES), ("RF", "yf", "PF", (0,)), ("G", "zp", "TN", (1,)),
]
REVERSED = ("B1", "B2", "B3", "B4", "XB", "KB", "LB", "FB")
ROWS = tuple(n for n, k, d, s in ROW)
COARSE = ROWS + ("XS",)
LAST = ("TF", "TN", "PF", "PN", "RF", "G")


PRIO = {
    "A1": -6.5, "A2": 4.7, "A3": 7.6, "A4": -4.8, "B1": 6.7, "B2": 1.6, "B3": 0.1, "B4": -0.4,
    "FA": -0.8, "FB": -3.4, "G": 0.2, "KA": -3.4, "KB": 4.8, "LA": -7.8, "LB": -4.8, "PF": -5.0,
    "PN": -7.0, "RF": 6.5, "TF": 1.8, "TN": 3.4, "XA": 1.7, "XB": 1.3, "XO": -7.7, "XS": -5.5,
    "YF": -2.0, "YN": -1.3,
}


def plan(table):
    unit, lat = 5.24 / PIECES, 2.2
    dep = {n: d for n, k, d, s in table}
    link = {(n, i): "w" if (n, i) in (("XA", 0), ("XB", 0)) else k for n, k, d, s in table for i in s}
    dur = {n: unit * (2 if n in COARSE else 1) for n in dep}

    def needs(m):
        n, i = m
        if dep[n] is None:
            return []
        if n in ("PF", "PN"):
            return [("A1", 2 * i), ("A1", 2 * i + 1)]
        return [(dep[n], i)]

    todo = list(link)
    tail = {}
    for m in reversed(todo):
        tail[m] = dur[m[0]] + lat + max([tail[o] for o in tail if m in needs(o)], default=0.0)
    free = {k: 0.0 for k in link.values()}
    done, start, now = {}, {}, 0.0
    while todo:
        for k in free:
            ready = [m for m in todo if link[m] == k and all(done.get(o, 1e9) <= now + 1e-9 for o in needs(m))]
            if free[k] <= now + 1e-9 and ready:
                m = min(ready, key=lambda m: (PRIO[m[0]] - tail[m], m[1]))
                todo.remove(m)
                start[m] = now
                done[m] = now + dur[m[0]] + lat
                free[k] = now + dur[m[0]]
        if todo:
            now = min(t for t in list(free.values()) + list(done.values()) if t > now + 1e-9)
    events = [(t, 0, m) for m, t in start.items()]
    events += [(done[m] + 0.3, 1, m) for m in start if m[0] in LAST]
    return [(kind, m, needs(m)) for t, kind, m in sorted(events)]


def kernel(band_hbm, mat_hbm, sign_hbm, square_hbm, left, right, cube, relay, mask_ref, acc, mat_ref, square_ref, sign_ref, band_ref,
           left_recv, sib_recv, right_recv, cube_recv, relay_recv, send_sems, local_sems):
    r = lax.axis_index("row")
    c = lax.axis_index("col")
    l = lax.axis_index("layer")
    tile = mat_hbm.shape[0]
    width = tile // 2
    count = tile // BLOCK
    piece = tile // PIECES
    x, zh = r // 4, r % 4
    y, zl = c // 2, c % 2
    ol = 1 - zl
    f = 1 - 2 * zl
    order = (0, 3, 1, 2)

    band_copy = pltpu.make_async_copy(band_hbm, band_ref, local_sems.at[0])
    band_copy.start()
    mat_copies = {}
    for p in order:
        rows = pl.ds(p * piece, piece)
        mat_copies[p] = pltpu.make_async_copy(mat_hbm.at[rows], mat_ref.at[rows], local_sems.at[1 + p])
        mat_copies[p].start()

    def at(dx=0, dzh=0, dy=0, zlow=zl):
        return (((x + dx + 4) % 4) * 4 + (zh + dzh + 4) % 4, ((y + dy + 8) % 8) * 2 + zlow, l)

    sibling = (r, c, 1 - l)
    xup, xdown = at(dx=1), at(dx=-1)
    device = {"zp": at(zlow=ol), "zo": at(dzh=-f, zlow=ol), "x": xup, "w": xdown, "yf": at(dy=f), "yn": at(dy=-f)}

    barrier = pltpu.get_barrier_semaphore()
    for other in (sibling, *device.values()):
        pl.semaphore_signal(barrier, inc=1, device_id=other, device_id_type=MESH)

    column = 4 * c + lax.broadcasted_iota(jnp.int32, (1, tile), 1) // BLOCK
    own_left = 4 + zl
    own_right = 4 + zh
    mine = pl.ds(pl.multiple_of(l * width, width), width)
    band_copy.wait()

    def own_piece(a):
        hit = column == band_ref[0, count * r + a]
        for j in range(1, band_ref.shape[0]):
            hit = hit | (column == band_ref[j, count * r + a])
        row_mask = jnp.where(hit, 1.0, 0.0).astype(jnp.float32)
        mask_ref[pl.ds(a, 1), :] = row_mask
        rows = pl.ds(a * BLOCK, BLOCK)
        mat_copies[a].wait()
        low = (mat_ref[rows, :] * row_mask).astype(jnp.bfloat16)
        left[own_left, 0, rows, :] = low[:, :width]
        left[own_left, 1, rows, :] = low[:, width:]
        right[own_right, rows, :] = left[own_left, l, rows, :]

    sent = []

    def remote(src, dst, recv_sem, target):
        return pltpu.make_async_remote_copy(
            src_ref=src, dst_ref=dst, send_sem=send_sems.at[len(sent)], recv_sem=recv_sem,
            device_id=target, device_id_type=MESH)

    def send(src, dst, recv_sem, target):
        copy = remote(src, dst, recv_sem, target)
        copy.start()
        sent.append((copy, None))

    def left_device(copies):
        for copy, only in copies:
            if only is None:
                copy.wait_send()
            else:
                pl.when(only)(copy.wait_send)

    def arrival(ref, sem):
        return pltpu.make_async_remote_copy(
            src_ref=ref, dst_ref=ref, send_sem=send_sems.at[0], recv_sem=sem,
            device_id=sibling, device_id_type=MESH)

    def arrived(ref, sem):
        arrival(ref, sem).wait_recv()

    links = {n: k for n, k, d, s in COLUMN + ROW}
    left_slot = {"YF": 4 - 2 * f + zl, "YN": 4 + 2 * f + zl, "TF": 4 - 4 * f + zl, "TN": 4 + 4 * f + zl,
                 "PF": 4 - 2 * f + ol, "PN": 4 + 2 * f + ol, "RF": 4 - 4 * f + ol, "G": 4 - 4 * f + ol, "A1": 4 + ol}
    near_a, near_b, far = (zh - f + 4) % 4, (zh + f + 4) % 4, (zh + 2) % 4
    halves = [pl.ds(j * width, width) for j in range(2)]
    edge = (zh == 0) | (zh == 3)
    side = (jnp.where(zh < 2, xdown[0], xup[0]), c, l)

    def gather(buf, sem, square, make_piece):
        phase = 0 if square else 1
        waited, made = set(), set()

        def rows_of(name, i):
            if name in COARSE:
                return halves[i]
            p = PIECES - 1 - i if name in REVERSED else i
            return pl.ds(p * piece, piece)

        def ensure(name, i):
            for p in ((2 * i, 2 * i + 1) if name in COARSE else (PIECES - 1 - i if name in REVERSED else i,)):
                if p not in made:
                    made.add(p)
                    make_piece(p)
                    if len(made) == 1 and square:
                        pl.semaphore_wait(barrier, 7)

        def landing(name, i):
            if name in left_slot and (square or name != "A1"):
                slot = left_slot[name]
                return left.at[slot, l, rows_of(name, i)], left_recv.at[slot, i]
            if name in ("XA", "XB", "KA", "KB"):
                slot = 12 if name in ("XA", "XB") else 13
                return buf.at[slot, rows_of(name, i)], sem.at[slot, 0 if name in ("XA", "KA") else 1]
            if name in ("A1", "B1", "A3", "B3"):
                place = {"A1": 0, "B1": PIECES, "A3": 2 * PIECES, "B3": 2 * PIECES + 2}[name] + i
                return relay.at[phase, place], relay_recv.at[phase, place]
            slot = 4 + {"A2": near_a, "B2": near_b, "A4": far, "B4": far}[name]
            return buf.at[slot, rows_of(name, i)], sem.at[slot, i + (2 if name == "B4" else 0)]

        def wait(name, i):
            if (name, i) in waited:
                return
            waited.add((name, i))
            arrived(*landing(name, i))
            if name in left_slot and square:
                if name == "A1":
                    if (name, i ^ 1) not in waited:
                        return
                    i = i // 2
                ref = left.at[left_slot[name], l, halves[i]]
                send(ref, ref, sib_recv.at[left_slot[name], i], sibling)

        def away(name, i):
            if name in ("XO", "XS", "XA", "XB", "LA", "LB", "FA", "FB"):
                zs = {"A": near_a, "B": near_b}.get(name[1], zh) if name[0] != "F" else far
                higher = {"XO": zh < 2, "XS": zh >= 2}.get(name, zs > zh)
                slot = jnp.where(higher, zs, 8 + zs)
                target = jnp.where(higher, xup[0], xdown[0])
                index = i + (2 if name == "FB" else 0)
                if name in ("LA", "LB"):
                    target = side[0]
                if name in ("XA", "XB") and i == 0:
                    slot = jnp.where(edge, 12, slot)
                    target = jnp.where(edge, side[0], target)
                    index = jnp.where(edge, 0 if name == "XA" else 1, 0)
                return buf.at[slot, rows_of(name, i)], sem.at[slot, index], (target, c, l)
            if name in ("KA", "KB"):
                return *landing(name, i), side
            target = device[links[name]]
            if name == "A1" and square:
                return left.at[own_left, l, rows_of(name, i)], left_recv.at[own_left, i], target
            if name == "G":
                slot = left_slot["TN"]
                return left.at[slot, l, halves[i]], left_recv.at[slot, i], target
            if name in ("A1", "B1", "A3", "B3") or name in ROWS:
                return *landing(name, i), target
            slot = 4 + {"A2": zh, "B2": near_a, "A4": near_b, "B4": far}[name]
            return buf.at[slot, rows_of(name, i)], sem.at[slot, i + (2 if name == "B4" else 0)], target

        for kind, (name, i), needs in plan(COLUMN + ROW if square else COLUMN):
            if kind == 1:
                wait(name, i)
            elif name in ("KA", "KB", "LA", "LB"):
                source, recv = landing(*needs[0])
                before = arrival(source, recv)
                copy = remote(source, *away(name, i))
                sent.append((copy, edge))

                @pl.when(edge)
                def _():
                    before.wait_recv()
                    copy.start()
            else:
                for m in needs:
                    wait(*m)
                if name in ROWS and needs:
                    source = left.at[left_slot[needs[0][0]], l, halves[i]]
                elif needs:
                    source = landing(*needs[0])[0]
                else:
                    ensure(name, i)
                    source = left.at[own_left, l, halves[i]] if name in ROWS else buf.at[own_right, rows_of(name, i)]
                send(source, *away(name, i))

    def gather_end(buf, sem):
        for i in range(PIECES):
            slot = jnp.where(zh < 2, zh, 8 + zh)
            arrived(buf.at[slot, pl.ds(i * piece, piece)], sem.at[slot, i])
        for i in range(2):
            slot = jnp.where(zh < 2, 8 + zh, zh)
            arrived(buf.at[slot, halves[i]], sem.at[slot, i])
        slot = jnp.where(far > zh, far, 8 + far)
        for i in range(2):
            arrived(buf.at[slot, pl.ds(i * piece, piece)], sem.at[slot, i])
            arrived(buf.at[slot, pl.ds((PIECES - 1 - i) * piece, piece)], sem.at[slot, i + 2])
        for i in range(PIECES):
            for p, zs in ((i, near_a), (PIECES - 1 - i, near_b)):
                slot = jnp.where(zs > zh, zs, 8 + zs)
                arrived(buf.at[slot, pl.ds(p * piece, piece)], sem.at[slot, i])

    first = jnp.maximum(jnp.maximum(r, c) - REACH, 0)
    stop = jnp.minimum(jnp.minimum(r, c) + REACH, 15) + 1
    inside = (c - r <= REACH) & (r - c <= REACH)
    stop = jnp.where(inside, stop, first)
    plane = 4 * x

    def product(buf, rows, chosen):
        def body(k, carry):
            @pl.when(chosen(k))
            def _():
                ls = k - c + zl + 4
                rs = k - r + zh + 4
                acc[rows, :] += jnp.dot(
                    left[ls, 0, rows, :], buf[rs, :width, :], preferred_element_type=jnp.float32) + jnp.dot(
                    left[ls, 1, rows, :], buf[rs, width:, :], preferred_element_type=jnp.float32)
            return carry

        lax.fori_loop(first, stop, body, 0)

    def in_plane(k):
        return (k >= plane) & (k < plane + 4)

    def early_left(k):
        return in_plane(k) & (k != c - 3 * f) & (k != c - 4 * f)

    def later(chosen):
        return lambda k: jnp.logical_not(chosen(k))

    def square_piece(a):
        rows = pl.ds(a * BLOCK, BLOCK)
        product(right, rows, later(early_left))
        value = acc[rows, :] * mask_ref[pl.ds(a, 1), mine]
        square_ref[rows, :] = value
        cube[own_right, rows, :] = value.astype(jnp.bfloat16)
        acc[rows, :] = jnp.zeros((BLOCK, width), jnp.float32)

    gather(right, right_recv, True, own_piece)
    acc[...] = jnp.zeros_like(acc)

    def from_sibling(names):
        for name in names:
            for j in ((0, 1) if name != "RF" else (0,)) if name != "G" else (1,):
                arrived(left.at[left_slot[name], 1 - l, halves[j]], sib_recv.at[left_slot[name], j])

    from_sibling(("A1", "YF", "YN", "PF", "PN", "TN"))
    for rows in halves:
        product(right, rows, early_left)
    from_sibling(("TF", "RF", "G"))
    gather_end(right, right_recv)

    early = len(sent)
    gather(cube, cube_recv, False, square_piece)
    square_copy = pltpu.make_async_copy(square_ref, square_hbm, local_sems.at[0])
    square_copy.start()
    left_device(sent[:early])
    for rows in halves:
        product(cube, rows, in_plane)
    gather_end(cube, cube_recv)
    sign_copies = []
    for j, rows in enumerate(halves):
        product(cube, rows, later(in_plane))
        for a in range(j * count // 2, (j + 1) * count // 2):
            block = pl.ds(a * BLOCK, BLOCK)
            row_mask = mask_ref[pl.ds(a, 1), mine]
            sparse = mat_ref[block, mine] * row_mask
            sign_ref[block, :] = row_mask * (1.5 * sparse - 0.5 * acc[block, :])
        sign_copies.append(pltpu.make_async_copy(sign_ref.at[rows], sign_hbm.at[rows], local_sems.at[1 + j]))
        sign_copies[-1].start()

    left_device(sent[early:])
    square_copy.wait()
    for copy in sign_copies:
        copy.wait()


def per_device(matrix, band_cols):
    tile = matrix.shape[0]
    width = tile // 2
    piece = tile // PIECES
    out = jax.ShapeDtypeStruct((tile, width), jnp.float32)
    return pl.pallas_call(
        kernel,
        out_shape=(out, out),
        in_specs=[pl.BlockSpec(memory_space=pltpu.HBM)] * 2,
        out_specs=(pl.BlockSpec(memory_space=pltpu.HBM),) * 2,
        scratch_shapes=[
            pltpu.VMEM((10, 2, tile, width), jnp.bfloat16),
            pltpu.VMEM((14, tile, width), jnp.bfloat16),
            pltpu.VMEM((14, tile, width), jnp.bfloat16),
            pltpu.VMEM((2, 3 * PIECES, piece, width), jnp.bfloat16),
            pltpu.VMEM((8, tile), jnp.float32),
            pltpu.VMEM((tile, width), jnp.float32),
            pltpu.VMEM((tile, tile), jnp.float32),
            pltpu.VMEM((tile, width), jnp.float32),
            pltpu.VMEM((tile, width), jnp.float32),
            pltpu.SMEM(band_cols.shape[::-1], jnp.int32),
            pltpu.SemaphoreType.DMA((10, PIECES)),
            pltpu.SemaphoreType.DMA((10, 2)),
            pltpu.SemaphoreType.DMA((14, PIECES)),
            pltpu.SemaphoreType.DMA((14, PIECES)),
            pltpu.SemaphoreType.DMA((2, 3 * PIECES)),
            pltpu.SemaphoreType.DMA((128,)),
            pltpu.SemaphoreType.DMA((1 + PIECES,)),
        ],
        compiler_params=pltpu.CompilerParams(
            collective_id=0, has_side_effects=True, vmem_limit_bytes=48 * 2**20),
        cost_estimate=pl.CostEstimate(flops=4 * 10**9, bytes_accessed=2 * 2**20, transcendentals=0),
    )(band_cols.T, matrix)


def solution(mesh):
    in_specs = (P("row", "col"), P())
    out_specs = (P("row", ("col", "layer")), P("row", ("col", "layer")))
    return jax.shard_map(
        per_device, mesh=mesh, in_specs=in_specs, out_specs=out_specs, check_vma=False
    )
```

```python
import jax
import jax.numpy as jnp
from jax import lax
from jax.experimental import pallas as pl
from jax.experimental.pallas import tpu as pltpu
from jax.sharding import PartitionSpec as P

BLOCK = 128
REACH = 4
PIECES = 4
MESH = pl.DeviceIdType.MESH
NEEDS = {"A2": "A1", "B2": "B1", "A3": "A2", "B3": "B2", "A4": "A3", "B4": "B3", "XA": "A2", "XB": "B2", "KA": "XA", "KB": "XB",
         "LA": "KA", "LB": "KB", "FA": "A4", "FB": "B4", "TF": "YF", "TN": "YN", "PF": "A1", "PN": "A1", "RF": "PF", "G": "TN"}
LINKS = {"A1": "zp", "B1": "zo", "A2": "zo", "B2": "zp", "A3": "zp", "B3": "zo", "A4": "zo", "B4": "zp", "YF": "yf", "YN": "yn",
         "TF": "yf", "TN": "yn", "PF": "yf", "PN": "yn", "RF": "yf", "G": "zp"}
REVERSED = ("B1", "B2", "B3", "B4", "XB", "KB", "LB", "FB")
ROWS = ("YF", "YN", "TF", "TN", "PF", "PN", "RF", "G")
COARSE = ROWS + ("XS",)
SQUARE_ORDER = (
    "A10", "B13", "YF0", "A11", "B11", "YF1", "XO0", "B10", "A13", "XO3", "YN1", "A20", "A12", "YN0",
    "B12", "B21", "A21", "XS1", "TF0", "XO2", "B20", "PF0", "B23", "TN1", "XO1", "A22", "XA0", "A23",
    "A30", "XB1", "PN0", "B31", "TF1", "XA1", "A31", "XB0", "PF1", "B30", "PN1", "B22", "XB3", "XS0",
    "XA2", "KA0", "A40", "XA3", "A41", "B41", "TN0", "?TF0", "RF0", "KB0", "XB2", "B40", "G1", "?TF1",
    "FA0", "?PN1", "FA1", "LA0", "?PF0", "FB1", "?TN0", "LB0", "?PF1", "?TN1", "FB0", "?G1", "?RF0", "?PN0",
)
CUBE_ORDER = (
    "A10", "B10", "XO0", "XS0", "A11", "B11", "XO1", "A12", "B12", "XO2", "XS1", "A13", "A20", "XO3",
    "A21", "B20", "B13", "B21", "XA0", "A22", "B22", "XA1", "XB0", "A30", "B30", "XB1", "B23", "B31",
    "KA0", "XB2", "A23", "A31", "KB0", "XA2", "A40", "B40", "XB3", "B41", "LA0", "A41", "XA3", "LB0",
    "FB0", "FB1", "FA0", "FA1",
)


def kernel(band_hbm, mat_hbm, sign_hbm, square_hbm, left, right, cube, relay, mask_ref, acc, mat_ref, square_ref, sign_ref, band_ref,
           left_recv, sib_recv, right_recv, cube_recv, relay_recv, send_sems, local_sems):
    r = lax.axis_index("row")
    c = lax.axis_index("col")
    l = lax.axis_index("layer")
    tile = mat_hbm.shape[0]
    width = tile // 2
    count = tile // BLOCK
    piece = tile // PIECES
    x, zh = r // 4, r % 4
    y, zl = c // 2, c % 2
    ol = 1 - zl
    f = 1 - 2 * zl
    order = (0, 3, 1, 2)

    band_copy = pltpu.make_async_copy(band_hbm, band_ref, local_sems.at[0])
    band_copy.start()
    mat_copies = {}
    for p in order:
        rows = pl.ds(p * piece, piece)
        mat_copies[p] = pltpu.make_async_copy(mat_hbm.at[rows], mat_ref.at[rows], local_sems.at[1 + p])
        mat_copies[p].start()

    def at(dx=0, dzh=0, dy=0, zlow=zl):
        return (((x + dx + 4) % 4) * 4 + (zh + dzh + 4) % 4, ((y + dy + 8) % 8) * 2 + zlow, l)

    sibling = (r, c, 1 - l)
    xup, xdown = at(dx=1), at(dx=-1)
    device = {"zp": at(zlow=ol), "zo": at(dzh=-f, zlow=ol), "x": xup, "w": xdown, "yf": at(dy=f), "yn": at(dy=-f)}

    barrier = pltpu.get_barrier_semaphore()
    for other in (sibling, *device.values()):
        pl.semaphore_signal(barrier, inc=1, device_id=other, device_id_type=MESH)

    column = 4 * c + lax.broadcasted_iota(jnp.int32, (1, tile), 1) // BLOCK
    own_left = 4 + zl
    own_right = 4 + zh
    mine = pl.ds(pl.multiple_of(l * width, width), width)
    band_copy.wait()

    def own_piece(a):
        hit = column == band_ref[0, count * r + a]
        for j in range(1, band_ref.shape[0]):
            hit = hit | (column == band_ref[j, count * r + a])
        row_mask = jnp.where(hit, 1.0, 0.0).astype(jnp.float32)
        mask_ref[pl.ds(a, 1), :] = row_mask
        rows = pl.ds(a * BLOCK, BLOCK)
        mat_copies[a].wait()
        low = (mat_ref[rows, :] * row_mask).astype(jnp.bfloat16)
        left[own_left, 0, rows, :] = low[:, :width]
        left[own_left, 1, rows, :] = low[:, width:]
        right[own_right, rows, :] = left[own_left, l, rows, :]

    sent = []

    def remote(src, dst, recv_sem, target):
        return pltpu.make_async_remote_copy(
            src_ref=src, dst_ref=dst, send_sem=send_sems.at[len(sent)], recv_sem=recv_sem,
            device_id=target, device_id_type=MESH)

    def send(src, dst, recv_sem, target):
        copy = remote(src, dst, recv_sem, target)
        copy.start()
        sent.append((copy, None))

    def left_device(copies):
        for copy, only in copies:
            if only is None:
                copy.wait_send()
            else:
                pl.when(only)(copy.wait_send)

    def arrival(ref, sem):
        return pltpu.make_async_remote_copy(
            src_ref=ref, dst_ref=ref, send_sem=send_sems.at[0], recv_sem=sem,
            device_id=sibling, device_id_type=MESH)

    def arrived(ref, sem):
        arrival(ref, sem).wait_recv()

    left_slot = {"YF": 4 - 2 * f + zl, "YN": 4 + 2 * f + zl, "TF": 4 - 4 * f + zl, "TN": 4 + 4 * f + zl,
                 "PF": 4 - 2 * f + ol, "PN": 4 + 2 * f + ol, "RF": 4 - 4 * f + ol, "G": 4 - 4 * f + ol, "A1": 4 + ol}
    near_a, near_b, far = (zh - f + 4) % 4, (zh + f + 4) % 4, (zh + 2) % 4
    halves = [pl.ds(j * width, width) for j in range(2)]
    edge = (zh == 0) | (zh == 3)
    side = (jnp.where(zh < 2, xdown[0], xup[0]), c, l)

    def gather(buf, sem, square, make_piece):
        phase = 0 if square else 1
        waited, made = set(), set()

        def rows_of(name, i):
            if name in COARSE:
                return halves[i]
            p = PIECES - 1 - i if name in REVERSED else i
            return pl.ds(p * piece, piece)

        def ensure(name, i):
            for p in ((2 * i, 2 * i + 1) if name in COARSE else (PIECES - 1 - i if name in REVERSED else i,)):
                if p not in made:
                    made.add(p)
                    make_piece(p)
                    if len(made) == 1 and square:
                        pl.semaphore_wait(barrier, 1 + len(device))

        def landing(name, i):
            if name in left_slot and (square or name != "A1"):
                slot = left_slot[name]
                return left.at[slot, l, rows_of(name, i)], left_recv.at[slot, i]
            if name in ("XA", "XB", "KA", "KB"):
                slot = 12 if name in ("XA", "XB") else 13
                return buf.at[slot, rows_of(name, i)], sem.at[slot, 0 if name in ("XA", "KA") else 1]
            if name in ("A1", "B1", "A3", "B3"):
                place = {"A1": 0, "B1": PIECES, "A3": 2 * PIECES, "B3": 2 * PIECES + 2}[name] + i
                return relay.at[phase, place], relay_recv.at[phase, place]
            slot = 4 + {"A2": near_a, "B2": near_b, "A4": far, "B4": far}[name]
            return buf.at[slot, rows_of(name, i)], sem.at[slot, i + (2 if name == "B4" else 0)]

        def wait(name, i):
            if (name, i) in waited:
                return
            waited.add((name, i))
            arrived(*landing(name, i))
            if name in left_slot and square:
                if name == "A1":
                    if (name, i ^ 1) not in waited:
                        return
                    i = i // 2
                ref = left.at[left_slot[name], l, halves[i]]
                send(ref, ref, sib_recv.at[left_slot[name], i], sibling)

        def away(name, i):
            if name in ("XO", "XS", "XA", "XB", "LA", "LB", "FA", "FB"):
                zs = {"A": near_a, "B": near_b}.get(name[1], zh) if name[0] != "F" else far
                higher = {"XO": zh < 2, "XS": zh >= 2}.get(name, zs > zh)
                slot = jnp.where(higher, zs, 8 + zs)
                target = jnp.where(higher, xup[0], xdown[0])
                index = i + (2 if name == "FB" else 0)
                if name in ("LA", "LB"):
                    target = side[0]
                if name in ("XA", "XB") and i == 0:
                    slot = jnp.where(edge, 12, slot)
                    target = jnp.where(edge, side[0], target)
                    index = jnp.where(edge, 0 if name == "XA" else 1, 0)
                return buf.at[slot, rows_of(name, i)], sem.at[slot, index], (target, c, l)
            if name in ("KA", "KB"):
                return *landing(name, i), side
            target = device[LINKS[name]]
            if name == "A1" and square:
                return left.at[own_left, l, rows_of(name, i)], left_recv.at[own_left, i], target
            if name == "G":
                slot = left_slot["TN"]
                return left.at[slot, l, halves[i]], left_recv.at[slot, i], target
            if name in ("A1", "B1", "A3", "B3") or name in ROWS:
                return *landing(name, i), target
            slot = 4 + {"A2": zh, "B2": near_a, "A4": near_b, "B4": far}[name]
            return buf.at[slot, rows_of(name, i)], sem.at[slot, i + (2 if name == "B4" else 0)], target

        for token in SQUARE_ORDER if square else CUBE_ORDER:
            name, i = token[:-1].lstrip("?"), int(token[-1])
            needs = [(NEEDS[name], i)] if NEEDS.get(name) else []
            if name in ("PF", "PN"):
                needs = [("A1", 2 * i), ("A1", 2 * i + 1)]
            if token[0] == "?":
                wait(name, i)
            elif name in ("KA", "KB", "LA", "LB"):
                source, recv = landing(*needs[0])
                before = arrival(source, recv)
                copy = remote(source, *away(name, i))
                sent.append((copy, edge))

                @pl.when(edge)
                def _():
                    before.wait_recv()
                    copy.start()
            else:
                for m in needs:
                    wait(*m)
                if name in ROWS and needs:
                    source = left.at[left_slot[needs[0][0]], l, halves[i]]
                elif needs:
                    source = landing(*needs[0])[0]
                else:
                    ensure(name, i)
                    source = left.at[own_left, l, halves[i]] if name in ROWS else buf.at[own_right, rows_of(name, i)]
                send(source, *away(name, i))

    def own_arrived(buf, sem):
        for i in range(PIECES):
            slot = jnp.where(zh < 2, zh, 8 + zh)
            arrived(buf.at[slot, pl.ds(i * piece, piece)], sem.at[slot, i])
        for i in range(2):
            slot = jnp.where(zh < 2, 8 + zh, zh)
            arrived(buf.at[slot, halves[i]], sem.at[slot, i])

    def near_arrived(buf, sem):
        for i in range(PIECES):
            for p, zs in ((i, near_a), (PIECES - 1 - i, near_b)):
                slot = jnp.where(zs > zh, zs, 8 + zs)
                arrived(buf.at[slot, pl.ds(p * piece, piece)], sem.at[slot, i])

    def far_arrived(buf, sem):
        slot = jnp.where(far > zh, far, 8 + far)
        for i in range(2):
            arrived(buf.at[slot, pl.ds(i * piece, piece)], sem.at[slot, i])
            arrived(buf.at[slot, pl.ds((PIECES - 1 - i) * piece, piece)], sem.at[slot, i + 2])

    first = jnp.maximum(jnp.maximum(r, c) - REACH, 0)
    stop = jnp.minimum(jnp.minimum(r, c) + REACH, 15) + 1
    inside = (c - r <= REACH) & (r - c <= REACH)
    stop = jnp.where(inside, stop, first)
    plane = 4 * x

    def product(buf, rows, chosen):
        def body(k, carry):
            @pl.when(chosen(k))
            def _():
                ls = k - c + zl + 4
                rs = k - r + zh + 4
                acc[rows, :] += jnp.dot(
                    left[ls, 0, rows, :], buf[rs, :width, :], preferred_element_type=jnp.float32) + jnp.dot(
                    left[ls, 1, rows, :], buf[rs, width:, :], preferred_element_type=jnp.float32)
            return carry

        lax.fori_loop(first, stop, body, 0)

    far_k = jnp.where(far > zh, plane - 4 + far, plane + 4 + far)

    def early(k):
        return ((k >= plane) & (k < plane + 4)) | (k == r - 4) | (k == r + 4)

    def early_both(k):
        return early(k) & (k != c + 3 * f) & (k != c - 3 * f)

    def is_far(k):
        return k == far_k

    def middle(chosen):
        return lambda k: jnp.logical_not(chosen(k) | is_far(k))

    def square_piece(a):
        rows = pl.ds(a * BLOCK, BLOCK)
        product(right, rows, is_far)
        value = acc[rows, :] * mask_ref[pl.ds(a, 1), mine]
        square_ref[rows, :] = value
        cube[own_right, rows, :] = value.astype(jnp.bfloat16)
        acc[rows, :] = jnp.zeros((BLOCK, width), jnp.float32)

    gather(right, right_recv, True, own_piece)
    acc[...] = jnp.zeros_like(acc)

    def from_sibling(names):
        for name in names:
            for j in ((0, 1) if name != "RF" else (0,)) if name != "G" else (1,):
                arrived(left.at[left_slot[name], 1 - l, halves[j]], sib_recv.at[left_slot[name], j])

    from_sibling(("A1", "YF", "YN", "PF", "TF", "TN"))
    own_arrived(right, right_recv)
    for rows in halves:
        product(right, rows, early_both)
    from_sibling(("PN", "RF", "G"))
    near_arrived(right, right_recv)
    for rows in halves:
        product(right, rows, middle(early_both))
    far_arrived(right, right_recv)

    started = len(sent)
    gather(cube, cube_recv, False, square_piece)
    square_copy = pltpu.make_async_copy(square_ref, square_hbm, local_sems.at[0])
    square_copy.start()
    left_device(sent[:started])
    own_arrived(cube, cube_recv)
    for rows in halves:
        product(cube, rows, early)
    near_arrived(cube, cube_recv)
    for rows in halves:
        product(cube, rows, middle(early))
    far_arrived(cube, cube_recv)
    sign_copies = []
    for j, rows in enumerate(halves):
        product(cube, rows, is_far)
        for a in range(j * count // 2, (j + 1) * count // 2):
            block = pl.ds(a * BLOCK, BLOCK)
            row_mask = mask_ref[pl.ds(a, 1), mine]
            sparse = mat_ref[block, mine] * row_mask
            sign_ref[block, :] = row_mask * (1.5 * sparse - 0.5 * acc[block, :])
        sign_copies.append(pltpu.make_async_copy(sign_ref.at[rows], sign_hbm.at[rows], local_sems.at[1 + j]))
        sign_copies[-1].start()

    left_device(sent[started:])
    square_copy.wait()
    for copy in sign_copies:
        copy.wait()


def per_device(matrix, band_cols):
    tile = matrix.shape[0]
    width = tile // 2
    piece = tile // PIECES
    out = jax.ShapeDtypeStruct((tile, width), jnp.float32)
    return pl.pallas_call(
        kernel,
        out_shape=(out, out),
        in_specs=[pl.BlockSpec(memory_space=pltpu.HBM)] * 2,
        out_specs=(pl.BlockSpec(memory_space=pltpu.HBM),) * 2,
        scratch_shapes=[
            pltpu.VMEM((10, 2, tile, width), jnp.bfloat16),
            pltpu.VMEM((14, tile, width), jnp.bfloat16),
            pltpu.VMEM((14, tile, width), jnp.bfloat16),
            pltpu.VMEM((2, 3 * PIECES, piece, width), jnp.bfloat16),
            pltpu.VMEM((8, tile), jnp.float32),
            pltpu.VMEM((tile, width), jnp.float32),
            pltpu.VMEM((tile, tile), jnp.float32),
            pltpu.VMEM((tile, width), jnp.float32),
            pltpu.VMEM((tile, width), jnp.float32),
            pltpu.SMEM(band_cols.shape[::-1], jnp.int32),
            pltpu.SemaphoreType.DMA((10, PIECES)),
            pltpu.SemaphoreType.DMA((10, 2)),
            pltpu.SemaphoreType.DMA((14, PIECES)),
            pltpu.SemaphoreType.DMA((14, PIECES)),
            pltpu.SemaphoreType.DMA((2, 3 * PIECES)),
            pltpu.SemaphoreType.DMA((128,)),
            pltpu.SemaphoreType.DMA((1 + PIECES,)),
        ],
        compiler_params=pltpu.CompilerParams(
            collective_id=0, has_side_effects=True, vmem_limit_bytes=105 * 2**19),
        cost_estimate=pl.CostEstimate(flops=4 * 10**9, bytes_accessed=2 * 2**20, transcendentals=0),
    )(band_cols.T, matrix)


def solution(mesh):
    in_specs = (P("row", "col"), P())
    out_specs = (P("row", ("col", "layer")), P("row", ("col", "layer")))
    return jax.shard_map(
        per_device, mesh=mesh, in_specs=in_specs, out_specs=out_specs, check_vma=False
    )
```

```python
import jax
import jax.numpy as jnp
from jax import lax
from jax.experimental import pallas as pl
from jax.experimental.pallas import tpu as pltpu
from jax.sharding import PartitionSpec as P

BLOCK = 128
REACH = 4
PIECES = 4
MESH = pl.DeviceIdType.MESH
NEEDS = {"A2": "A1", "B2": "B1", "A3": "A2", "B3": "B2", "A4": "A3", "B4": "B3", "XA": "A2", "XB": "B2", "KA": "XA", "KB": "XB",
         "LA": "KA", "LB": "KB", "FA": "A4", "FB": "B4", "TF": "YF", "TN": "YN", "PF": "A1", "PN": "A1", "RF": "PF", "G": "TN"}
LINKS = {"A1": "zp", "B1": "zo", "A2": "zo", "B2": "zp", "A3": "zp", "B3": "zo", "A4": "zo", "B4": "zp", "YF": "yf", "YN": "yn",
         "TF": "yf", "TN": "yn", "PF": "yf", "PN": "yn", "RF": "yf", "G": "zp"}
REVERSED = ("B1", "B2", "B3", "B4", "XB", "KB", "LB", "FB")
ROWS = ("YF", "YN", "TF", "TN", "PF", "PN", "RF", "G")
COARSE = ROWS + ("XS",)
SQUARE_ORDER = (
    "A10", "B13", "YF0", "A11", "B11", "YF1", "XO0", "B10", "A13", "XO3", "YN1", "A20", "A12", "YN0",
    "B12", "B21", "A21", "XS1", "TF0", "XO2", "B20", "PF0", "B23", "TN1", "XO1", "A22", "XA0", "A23",
    "A30", "XB1", "PN0", "B31", "TF1", "XA1", "A31", "XB0", "PF1", "B30", "PN1", "B22", "XB3", "XS0",
    "XA2", "KA0", "A40", "XA3", "A41", "B41", "TN0", "?TF0", "RF0", "KB0", "XB2", "B40", "G1", "?TF1",
    "FA0", "?PN1", "FA1", "LA0", "?PF0", "FB1", "?TN0", "LB0", "?PF1", "?TN1", "FB0", "?G1", "?RF0", "?PN0",
)
CUBE_ORDER = (
    "A10", "B10", "XO0", "XS0", "A11", "B11", "XO1", "A12", "B12", "XO2", "XS1", "A13", "A20", "XO3",
    "A21", "B20", "B13", "B21", "XA0", "A22", "B22", "XA1", "XB0", "A30", "B30", "XB1", "B23", "B31",
    "KA0", "XB2", "A23", "A31", "KB0", "XA2", "A40", "B40", "XB3", "B41", "LA0", "A41", "XA3", "LB0",
    "FB0", "FB1", "FA0", "FA1",
)


def kernel(band_hbm, mat_hbm, sign_hbm, square_hbm, left, right, cube, relay, mask_ref, acc, mat_ref, square_ref, sign_ref, band_ref,
           left_recv, sib_recv, right_recv, cube_recv, relay_recv, send_sems, local_sems):
    r = lax.axis_index("row")
    c = lax.axis_index("col")
    l = lax.axis_index("layer")
    tile = mat_hbm.shape[0]
    width = tile // 2
    count = tile // BLOCK
    piece = tile // PIECES
    x, zh = r // 4, r % 4
    y, zl = c // 2, c % 2
    ol = 1 - zl
    f = 1 - 2 * zl
    order = (0, 3, 1, 2)

    band_copy = pltpu.make_async_copy(band_hbm, band_ref, local_sems.at[0])
    band_copy.start()
    mat_copies = {}
    for p in order:
        rows = pl.ds(p * piece, piece)
        mat_copies[p] = pltpu.make_async_copy(mat_hbm.at[rows], mat_ref.at[rows], local_sems.at[1 + p])
        mat_copies[p].start()

    def at(dx=0, dzh=0, dy=0, zlow=zl):
        return (((x + dx + 4) % 4) * 4 + (zh + dzh + 4) % 4, ((y + dy + 8) % 8) * 2 + zlow, l)

    sibling = (r, c, 1 - l)
    xup, xdown = at(dx=1), at(dx=-1)
    device = {"zp": at(zlow=ol), "zo": at(dzh=-f, zlow=ol), "x": xup, "w": xdown, "yf": at(dy=f), "yn": at(dy=-f)}

    barrier = pltpu.get_barrier_semaphore()
    for other in (sibling, *device.values()):
        pl.semaphore_signal(barrier, inc=1, device_id=other, device_id_type=MESH)

    column = 4 * c + lax.broadcasted_iota(jnp.int32, (1, tile), 1) // BLOCK
    own_left = 4 + zl
    own_right = 4 + zh
    mine = pl.ds(pl.multiple_of(l * width, width), width)
    band_copy.wait()

    def own_piece(a):
        hit = column == band_ref[0, count * r + a]
        for j in range(1, band_ref.shape[0]):
            hit = hit | (column == band_ref[j, count * r + a])
        row_mask = jnp.where(hit, 1.0, 0.0).astype(jnp.float32)
        mask_ref[pl.ds(a, 1), :] = row_mask
        rows = pl.ds(a * BLOCK, BLOCK)
        mat_copies[a].wait()
        low = (mat_ref[rows, :] * row_mask).astype(jnp.bfloat16)
        left[own_left, 0, rows, :] = low[:, :width]
        left[own_left, 1, rows, :] = low[:, width:]
        right[own_right, rows, :] = left[own_left, l, rows, :]

    sent = []

    def remote(src, dst, recv_sem, target):
        return pltpu.make_async_remote_copy(
            src_ref=src, dst_ref=dst, send_sem=send_sems.at[len(sent)], recv_sem=recv_sem,
            device_id=target, device_id_type=MESH)

    def send(src, dst, recv_sem, target):
        copy = remote(src, dst, recv_sem, target)
        copy.start()
        sent.append((copy, None))

    def left_device(copies):
        for copy, only in copies:
            if only is None:
                copy.wait_send()
            else:
                pl.when(only)(copy.wait_send)

    def arrival(ref, sem):
        return pltpu.make_async_remote_copy(
            src_ref=ref, dst_ref=ref, send_sem=send_sems.at[0], recv_sem=sem,
            device_id=sibling, device_id_type=MESH)

    def arrived(ref, sem):
        arrival(ref, sem).wait_recv()

    left_slot = {"YF": 4 - 2 * f + zl, "YN": 4 + 2 * f + zl, "TF": 4 - 4 * f + zl, "TN": 4 + 4 * f + zl,
                 "PF": 4 - 2 * f + ol, "PN": 4 + 2 * f + ol, "RF": 4 - 4 * f + ol, "G": 4 - 4 * f + ol, "A1": 4 + ol}
    near_a, near_b, far = (zh - f + 4) % 4, (zh + f + 4) % 4, (zh + 2) % 4
    halves = [pl.ds(j * width, width) for j in range(2)]
    edge = (zh == 0) | (zh == 3)
    side = (jnp.where(zh < 2, xdown[0], xup[0]), c, l)

    def gather(buf, sem, square, make_piece):
        phase = 0 if square else 1
        waited, made = set(), set()

        def rows_of(name, i):
            if name in COARSE:
                return halves[i]
            p = PIECES - 1 - i if name in REVERSED else i
            return pl.ds(p * piece, piece)

        def ensure(name, i):
            for p in ((2 * i, 2 * i + 1) if name in COARSE else (PIECES - 1 - i if name in REVERSED else i,)):
                if p not in made:
                    made.add(p)
                    make_piece(p)
                    if len(made) == 1 and square:
                        pl.semaphore_wait(barrier, 1 + len(device))

        def landing(name, i):
            if name in left_slot and (square or name != "A1"):
                slot = left_slot[name]
                return left.at[slot, l, rows_of(name, i)], left_recv.at[slot, i]
            if name in ("XA", "XB", "KA", "KB"):
                slot = 12 if name in ("XA", "XB") else 13
                return buf.at[slot, rows_of(name, i)], sem.at[slot, 0 if name in ("XA", "KA") else 1]
            if name in ("A1", "B1", "A3", "B3"):
                place = {"A1": 0, "B1": PIECES, "A3": 2 * PIECES, "B3": 2 * PIECES + 2}[name] + i
                return relay.at[phase, place], relay_recv.at[phase, place]
            slot = 4 + {"A2": near_a, "B2": near_b, "A4": far, "B4": far}[name]
            return buf.at[slot, rows_of(name, i)], sem.at[slot, i + (2 if name == "B4" else 0)]

        def wait(name, i):
            if (name, i) in waited:
                return
            waited.add((name, i))
            arrived(*landing(name, i))
            if name in left_slot and square:
                if name == "A1":
                    if (name, i ^ 1) not in waited:
                        return
                    i = i // 2
                ref = left.at[left_slot[name], l, halves[i]]
                send(ref, ref, sib_recv.at[left_slot[name], i], sibling)

        def away(name, i):
            if name in ("XO", "XS", "XA", "XB", "LA", "LB", "FA", "FB"):
                zs = {"A": near_a, "B": near_b}.get(name[1], zh) if name[0] != "F" else far
                higher = {"XO": zh < 2, "XS": zh >= 2}.get(name, zs > zh)
                slot = jnp.where(higher, zs, 8 + zs)
                target = jnp.where(higher, xup[0], xdown[0])
                index = i + (2 if name == "FB" else 0)
                if name in ("LA", "LB"):
                    target = side[0]
                if name in ("XA", "XB") and i == 0:
                    slot = jnp.where(edge, 12, slot)
                    target = jnp.where(edge, side[0], target)
                    index = jnp.where(edge, 0 if name == "XA" else 1, 0)
                return buf.at[slot, rows_of(name, i)], sem.at[slot, index], (target, c, l)
            if name in ("KA", "KB"):
                return *landing(name, i), side
            target = device[LINKS[name]]
            if name == "A1" and square:
                return left.at[own_left, l, rows_of(name, i)], left_recv.at[own_left, i], target
            if name == "G":
                slot = left_slot["TN"]
                return left.at[slot, l, halves[i]], left_recv.at[slot, i], target
            if name in ("A1", "B1", "A3", "B3") or name in ROWS:
                return *landing(name, i), target
            slot = 4 + {"A2": zh, "B2": near_a, "A4": near_b, "B4": far}[name]
            return buf.at[slot, rows_of(name, i)], sem.at[slot, i + (2 if name == "B4" else 0)], target

        for token in SQUARE_ORDER if square else CUBE_ORDER:
            name, i = token[:-1].lstrip("?"), int(token[-1])
            needs = [(NEEDS[name], i)] if NEEDS.get(name) else []
            if name in ("PF", "PN"):
                needs = [("A1", 2 * i), ("A1", 2 * i + 1)]
            if token[0] == "?":
                wait(name, i)
            elif name in ("KA", "KB", "LA", "LB"):
                source, recv = landing(*needs[0])
                before = arrival(source, recv)
                copy = remote(source, *away(name, i))
                sent.append((copy, edge))

                @pl.when(edge)
                def _():
                    before.wait_recv()
                    copy.start()
            else:
                for m in needs:
                    wait(*m)
                if name in ROWS and needs:
                    source = left.at[left_slot[needs[0][0]], l, halves[i]]
                elif needs:
                    source = landing(*needs[0])[0]
                else:
                    ensure(name, i)
                    source = left.at[own_left, l, halves[i]] if name in ROWS else buf.at[own_right, rows_of(name, i)]
                send(source, *away(name, i))

    def own_arrived(buf, sem):
        for i in range(PIECES):
            slot = jnp.where(zh < 2, zh, 8 + zh)
            arrived(buf.at[slot, pl.ds(i * piece, piece)], sem.at[slot, i])
        for i in range(2):
            slot = jnp.where(zh < 2, 8 + zh, zh)
            arrived(buf.at[slot, halves[i]], sem.at[slot, i])

    def near_arrived(buf, sem):
        for i in range(PIECES):
            for p, zs in ((i, near_a), (PIECES - 1 - i, near_b)):
                slot = jnp.where(zs > zh, zs, 8 + zs)
                arrived(buf.at[slot, pl.ds(p * piece, piece)], sem.at[slot, i])

    def far_arrived(buf, sem):
        slot = jnp.where(far > zh, far, 8 + far)
        for i in range(2):
            arrived(buf.at[slot, pl.ds(i * piece, piece)], sem.at[slot, i])
            arrived(buf.at[slot, pl.ds((PIECES - 1 - i) * piece, piece)], sem.at[slot, i + 2])

    first = jnp.maximum(jnp.maximum(r, c) - REACH, 0)
    stop = jnp.minimum(jnp.minimum(r, c) + REACH, 15) + 1
    inside = (c - r <= REACH) & (r - c <= REACH)
    stop = jnp.where(inside, stop, first)
    plane = 4 * x

    def add_product(buf, rows, k):
        ls = k - c + zl + 4
        rs = k - r + zh + 4
        acc[rows, :] += jnp.dot(
            left[ls, 0, rows, :], buf[rs, :width, :], preferred_element_type=jnp.float32) + jnp.dot(
            left[ls, 1, rows, :], buf[rs, width:, :], preferred_element_type=jnp.float32)

    def product(buf, rows, chosen):
        def body(k, carry):
            pl.when(chosen(k))(lambda: add_product(buf, rows, k))
            return carry

        lax.fori_loop(first, stop, body, 0)

    def far_product(buf, rows):
        pl.when((far_k >= first) & (far_k < stop))(lambda: add_product(buf, rows, far_k))

    far_k = jnp.where(far > zh, plane - 4 + far, plane + 4 + far)

    def early(k):
        return ((k >= plane) & (k < plane + 4)) | (k == r - 4) | (k == r + 4)

    def early_both(k):
        return early(k) & (k != c + 3 * f) & (k != c - 3 * f)

    def middle(chosen):
        return lambda k: jnp.logical_not(chosen(k) | (k == far_k))

    def square_piece(a):
        rows = pl.ds(a * BLOCK, BLOCK)
        far_product(right, rows)
        value = acc[rows, :] * mask_ref[pl.ds(a, 1), mine]
        square_ref[rows, :] = value
        cube[own_right, rows, :] = value.astype(jnp.bfloat16)
        acc[rows, :] = jnp.zeros((BLOCK, width), jnp.float32)

    gather(right, right_recv, True, own_piece)
    acc[...] = jnp.zeros_like(acc)

    def from_sibling(names):
        for name in names:
            for j in ((0, 1) if name != "RF" else (0,)) if name != "G" else (1,):
                arrived(left.at[left_slot[name], 1 - l, halves[j]], sib_recv.at[left_slot[name], j])

    from_sibling(("A1", "YF", "YN", "PF", "TF", "TN"))
    own_arrived(right, right_recv)
    for rows in halves:
        product(right, rows, early_both)
    from_sibling(("PN", "RF", "G"))
    near_arrived(right, right_recv)
    for rows in halves:
        product(right, rows, middle(early_both))
    far_arrived(right, right_recv)

    started = len(sent)
    gather(cube, cube_recv, False, square_piece)
    square_copy = pltpu.make_async_copy(square_ref, square_hbm, local_sems.at[0])
    square_copy.start()
    left_device(sent[:started])
    own_arrived(cube, cube_recv)
    for rows in halves:
        product(cube, rows, early)
    near_arrived(cube, cube_recv)
    for rows in halves:
        product(cube, rows, middle(early))
    left_device(sent[started:])
    far_arrived(cube, cube_recv)
    sign_copies = []
    for j, rows in enumerate(halves):
        far_product(cube, rows)
        for a in range(j * count // 2, (j + 1) * count // 2):
            block = pl.ds(a * BLOCK, BLOCK)
            row_mask = mask_ref[pl.ds(a, 1), mine]
            sparse = mat_ref[block, mine] * row_mask
            sign_ref[block, :] = row_mask * (1.5 * sparse - 0.5 * acc[block, :])
        sign_copies.append(pltpu.make_async_copy(sign_ref.at[rows], sign_hbm.at[rows], local_sems.at[1 + j]))
        sign_copies[-1].start()

    square_copy.wait()
    for copy in sign_copies:
        copy.wait()


def per_device(matrix, band_cols):
    tile = matrix.shape[0]
    width = tile // 2
    piece = tile // PIECES
    out = jax.ShapeDtypeStruct((tile, width), jnp.float32)
    return pl.pallas_call(
        kernel,
        out_shape=(out, out),
        in_specs=[pl.BlockSpec(memory_space=pltpu.HBM)] * 2,
        out_specs=(pl.BlockSpec(memory_space=pltpu.HBM),) * 2,
        scratch_shapes=[
            pltpu.VMEM((10, 2, tile, width), jnp.bfloat16),
            pltpu.VMEM((14, tile, width), jnp.bfloat16),
            pltpu.VMEM((14, tile, width), jnp.bfloat16),
            pltpu.VMEM((2, 3 * PIECES, piece, width), jnp.bfloat16),
            pltpu.VMEM((8, tile), jnp.float32),
            pltpu.VMEM((tile, width), jnp.float32),
            pltpu.VMEM((tile, tile), jnp.float32),
            pltpu.VMEM((tile, width), jnp.float32),
            pltpu.VMEM((tile, width), jnp.float32),
            pltpu.SMEM(band_cols.shape[::-1], jnp.int32),
            pltpu.SemaphoreType.DMA((10, PIECES)),
            pltpu.SemaphoreType.DMA((10, 2)),
            pltpu.SemaphoreType.DMA((14, PIECES)),
            pltpu.SemaphoreType.DMA((14, PIECES)),
            pltpu.SemaphoreType.DMA((2, 3 * PIECES)),
            pltpu.SemaphoreType.DMA((128,)),
            pltpu.SemaphoreType.DMA((1 + PIECES,)),
        ],
        compiler_params=pltpu.CompilerParams(
            collective_id=0, has_side_effects=True, vmem_limit_bytes=105 * 2**19),
        cost_estimate=pl.CostEstimate(flops=4 * 10**9, bytes_accessed=2 * 2**20, transcendentals=0),
    )(band_cols.T, matrix)


def solution(mesh):
    in_specs = (P("row", "col"), P())
    out_specs = (P("row", ("col", "layer")), P("row", ("col", "layer")))
    return jax.shard_map(
        per_device, mesh=mesh, in_specs=in_specs, out_specs=out_specs, check_vma=False
    )
```

```python
import jax
import jax.numpy as jnp
from jax import lax
from jax.experimental import pallas as pl
from jax.experimental.pallas import tpu as pltpu
from jax.sharding import PartitionSpec as P

BLOCK = 128
REACH = 4
PIECES = 4
MESH = pl.DeviceIdType.MESH
NEEDS = {"A2": "A1", "B2": "B1", "A3": "A2", "B3": "B2", "A4": "A3", "B4": "B3", "XA": "A2", "XB": "B2", "KA": "XA", "KB": "XB",
         "LA": "KA", "LB": "KB", "FA": "A4", "FB": "B4", "TF": "YF", "TN": "YN", "PF": "A1", "PN": "A1", "RF": "PF", "G": "TN"}
LINKS = {"A1": "zp", "B1": "zo", "A2": "zo", "B2": "zp", "A3": "zp", "B3": "zo", "A4": "zo", "B4": "zp", "YF": "yf", "YN": "yn",
         "TF": "yf", "TN": "yn", "PF": "yf", "PN": "yn", "RF": "yf", "G": "zp"}
REVERSED = ("B1", "B2", "B3", "B4", "XB", "KB", "LB", "FB")
ROWS = ("YF", "YN", "TF", "TN", "PF", "PN", "RF", "G")
COARSE = ROWS + ("XS",)
SQUARE_ORDER = (
    "A10", "B13", "YF0", "A11", "B11", "YF1", "XO0", "B10", "A13", "XO3", "YN1", "A20", "A12", "YN0",
    "B12", "B21", "A21", "XS1", "TF0", "XO2", "B20", "PF0", "B23", "TN1", "XO1", "A22", "XA0", "A23",
    "A30", "XB1", "PN0", "B31", "TF1", "XA1", "A31", "XB0", "PF1", "B30", "PN1", "B22", "XB3", "XS0",
    "XA2", "KA0", "A40", "XA3", "A41", "B41", "TN0", "?TF0", "RF0", "KB0", "XB2", "B40", "G1", "?TF1",
    "FA0", "?PN1", "FA1", "LA0", "?PF0", "FB1", "?TN0", "LB0", "?PF1", "?TN1", "FB0", "?G1", "?RF0", "?PN0",
)
CUBE_ORDER = (
    "A10", "B10", "XO0", "XS0", "A11", "B11", "XO1", "A12", "B12", "XO2", "XS1", "A13", "A20", "XO3",
    "A21", "B20", "B13", "B21", "XA0", "A22", "B22", "XA1", "XB0", "A30", "B30", "XB1", "B23", "B31",
    "KA0", "XB2", "A23", "A31", "KB0", "XA2", "A40", "B40", "XB3", "B41", "LA0", "A41", "XA3", "LB0",
    "FB0", "FB1", "FA0", "FA1",
)


def kernel(band_hbm, mat_hbm, sign_hbm, square_hbm, left, right, cube, relay, mask_ref, acc, mat_ref, square_ref, sign_ref, band_ref,
           left_recv, sib_recv, right_recv, cube_recv, relay_recv, send_sems, local_sems):
    r = lax.axis_index("row")
    c = lax.axis_index("col")
    l = lax.axis_index("layer")
    tile = mat_hbm.shape[0]
    width = tile // 2
    count = tile // BLOCK
    piece = tile // PIECES
    x, zh = r // 4, r % 4
    y, zl = c // 2, c % 2
    ol = 1 - zl
    f = 1 - 2 * zl

    def at(dx=0, dzh=0, dy=0, zlow=zl):
        return (((x + dx + 4) % 4) * 4 + (zh + dzh + 4) % 4, ((y + dy + 8) % 8) * 2 + zlow, l)

    sibling = (r, c, 1 - l)
    xup, xdown = at(dx=1), at(dx=-1)
    device = {"zp": at(zlow=ol), "zo": at(dzh=-f, zlow=ol), "x": xup, "w": xdown, "yf": at(dy=f), "yn": at(dy=-f)}

    barrier = pltpu.get_barrier_semaphore()
    for other in (sibling, *device.values()):
        pl.semaphore_signal(barrier, inc=1, device_id=other, device_id_type=MESH)

    band_copy = pltpu.make_async_copy(band_hbm, band_ref, local_sems.at[0])
    band_copy.start()
    mat_copies = {}
    for p in range(PIECES):
        rows = pl.ds(p * piece, piece)
        mat_copies[p] = pltpu.make_async_copy(mat_hbm.at[rows], mat_ref.at[rows], local_sems.at[1 + p])
        mat_copies[p].start()

    column = 4 * c + lax.broadcasted_iota(jnp.int32, (1, tile), 1) // BLOCK
    own_left = 4 + zl
    own_right = 4 + zh
    mine = pl.ds(pl.multiple_of(l * width, width), width)
    band_copy.wait()

    def own_piece(a):
        hit = column == band_ref[0, count * r + a]
        for j in range(1, band_ref.shape[0]):
            hit = hit | (column == band_ref[j, count * r + a])
        row_mask = jnp.where(hit, 1.0, 0.0).astype(jnp.float32)
        mask_ref[pl.ds(a, 1), :] = row_mask
        rows = pl.ds(a * BLOCK, BLOCK)
        mat_copies[a].wait()
        low = (mat_ref[rows, :] * row_mask).astype(jnp.bfloat16)
        left[own_left, 0, rows, :] = low[:, :width]
        left[own_left, 1, rows, :] = low[:, width:]
        right[own_right, rows, :] = left[own_left, l, rows, :]

    sent = []

    def remote(src, dst, recv_sem, target):
        return pltpu.make_async_remote_copy(
            src_ref=src, dst_ref=dst, send_sem=send_sems.at[len(sent)], recv_sem=recv_sem,
            device_id=target, device_id_type=MESH)

    def send(src, dst, recv_sem, target):
        copy = remote(src, dst, recv_sem, target)
        copy.start()
        sent.append((copy, None))

    def left_device(copies):
        for copy, only in copies:
            if only is None:
                copy.wait_send()
            else:
                pl.when(only)(copy.wait_send)

    def arrival(ref, sem):
        return pltpu.make_async_remote_copy(
            src_ref=ref, dst_ref=ref, send_sem=send_sems.at[0], recv_sem=sem,
            device_id=sibling, device_id_type=MESH)

    def arrived(ref, sem):
        arrival(ref, sem).wait_recv()

    left_slot = {"YF": 4 - 2 * f + zl, "YN": 4 + 2 * f + zl, "TF": 4 - 4 * f + zl, "TN": 4 + 4 * f + zl,
                 "PF": 4 - 2 * f + ol, "PN": 4 + 2 * f + ol, "RF": 4 - 4 * f + ol, "G": 4 - 4 * f + ol, "A1": 4 + ol}
    near_a, near_b, far = (zh - f + 4) % 4, (zh + f + 4) % 4, (zh + 2) % 4
    halves = [pl.ds(j * width, width) for j in range(2)]
    edge = (zh == 0) | (zh == 3)
    side = (jnp.where(zh < 2, xdown[0], xup[0]), c, l)

    def gather(buf, sem, square, make_piece):
        phase = 0 if square else 1
        waited, made = set(), set()

        def rows_of(name, i):
            if name in COARSE:
                return halves[i]
            p = PIECES - 1 - i if name in REVERSED else i
            return pl.ds(p * piece, piece)

        def ensure(name, i):
            for p in ((2 * i, 2 * i + 1) if name in COARSE else (PIECES - 1 - i if name in REVERSED else i,)):
                if p not in made:
                    made.add(p)
                    make_piece(p)
                    if len(made) == 1 and square:
                        pl.semaphore_wait(barrier, 1 + len(device))

        def landing(name, i):
            if name in left_slot and (square or name != "A1"):
                slot = left_slot[name]
                return left.at[slot, l, rows_of(name, i)], left_recv.at[slot, i]
            if name in ("XA", "XB", "KA", "KB"):
                slot = 12 if name in ("XA", "XB") else 13
                return buf.at[slot, rows_of(name, i)], sem.at[slot, 0 if name in ("XA", "KA") else 1]
            if name in ("A1", "B1", "A3", "B3"):
                place = {"A1": 0, "B1": PIECES, "A3": 2 * PIECES, "B3": 2 * PIECES + 2}[name] + i
                return relay.at[phase, place], relay_recv.at[phase, place]
            slot = 4 + {"A2": near_a, "B2": near_b, "A4": far, "B4": far}[name]
            return buf.at[slot, rows_of(name, i)], sem.at[slot, i + (2 if name == "B4" else 0)]

        def wait(name, i):
            if (name, i) in waited:
                return
            waited.add((name, i))
            arrived(*landing(name, i))
            if name in left_slot and square:
                if name == "A1":
                    if (name, i ^ 1) not in waited:
                        return
                    i = i // 2
                ref = left.at[left_slot[name], l, halves[i]]
                send(ref, ref, sib_recv.at[left_slot[name], i], sibling)

        def away(name, i):
            if name in ("XO", "XS", "XA", "XB", "LA", "LB", "FA", "FB"):
                zs = {"A": near_a, "B": near_b}.get(name[1], zh) if name[0] != "F" else far
                higher = {"XO": zh < 2, "XS": zh >= 2}.get(name, zs > zh)
                slot = jnp.where(higher, zs, 8 + zs)
                target = jnp.where(higher, xup[0], xdown[0])
                index = i + (2 if name == "FB" else 0)
                if name in ("LA", "LB"):
                    target = side[0]
                if name in ("XA", "XB") and i == 0:
                    slot = jnp.where(edge, 12, slot)
                    target = jnp.where(edge, side[0], target)
                    index = jnp.where(edge, 0 if name == "XA" else 1, 0)
                return buf.at[slot, rows_of(name, i)], sem.at[slot, index], (target, c, l)
            if name in ("KA", "KB"):
                return *landing(name, i), side
            target = device[LINKS[name]]
            if name == "A1" and square:
                return left.at[own_left, l, rows_of(name, i)], left_recv.at[own_left, i], target
            if name == "G":
                slot = left_slot["TN"]
                return left.at[slot, l, halves[i]], left_recv.at[slot, i], target
            if name in ("A1", "B1", "A3", "B3") or name in ROWS:
                return *landing(name, i), target
            slot = 4 + {"A2": zh, "B2": near_a, "A4": near_b, "B4": far}[name]
            return buf.at[slot, rows_of(name, i)], sem.at[slot, i + (2 if name == "B4" else 0)], target

        for token in SQUARE_ORDER if square else CUBE_ORDER:
            name, i = token[:-1].lstrip("?"), int(token[-1])
            needs = [(NEEDS[name], i)] if NEEDS.get(name) else []
            if name in ("PF", "PN"):
                needs = [("A1", 2 * i), ("A1", 2 * i + 1)]
            if token[0] == "?":
                wait(name, i)
            elif name in ("KA", "KB", "LA", "LB"):
                source, recv = landing(*needs[0])
                before = arrival(source, recv)
                copy = remote(source, *away(name, i))
                sent.append((copy, edge))

                @pl.when(edge)
                def _():
                    before.wait_recv()
                    copy.start()
            else:
                for m in needs:
                    wait(*m)
                if name in ROWS and needs:
                    source = left.at[left_slot[needs[0][0]], l, halves[i]]
                elif needs:
                    source = landing(*needs[0])[0]
                else:
                    ensure(name, i)
                    source = left.at[own_left, l, halves[i]] if name in ROWS else buf.at[own_right, rows_of(name, i)]
                send(source, *away(name, i))

    def own_arrived(buf, sem):
        for i in range(PIECES):
            slot = jnp.where(zh < 2, zh, 8 + zh)
            arrived(buf.at[slot, pl.ds(i * piece, piece)], sem.at[slot, i])
        for i in range(2):
            slot = jnp.where(zh < 2, 8 + zh, zh)
            arrived(buf.at[slot, halves[i]], sem.at[slot, i])

    def near_arrived(buf, sem):
        for i in range(PIECES):
            for p, zs in ((i, near_a), (PIECES - 1 - i, near_b)):
                slot = jnp.where(zs > zh, zs, 8 + zs)
                arrived(buf.at[slot, pl.ds(p * piece, piece)], sem.at[slot, i])

    def far_arrived(buf, sem):
        slot = jnp.where(far > zh, far, 8 + far)
        for i in range(2):
            arrived(buf.at[slot, pl.ds(i * piece, piece)], sem.at[slot, i])
            arrived(buf.at[slot, pl.ds((PIECES - 1 - i) * piece, piece)], sem.at[slot, i + 2])

    first = jnp.maximum(jnp.maximum(r, c) - REACH, 0)
    stop = jnp.minimum(jnp.minimum(r, c) + REACH, 15) + 1
    inside = (c - r <= REACH) & (r - c <= REACH)
    stop = jnp.where(inside, stop, first)
    plane = 4 * x

    def add_product(buf, rows, k):
        ls = k - c + zl + 4
        rs = k - r + zh + 4
        acc[rows, :] += jnp.dot(
            left[ls, 0, rows, :], buf[rs, :width, :], preferred_element_type=jnp.float32) + jnp.dot(
            left[ls, 1, rows, :], buf[rs, width:, :], preferred_element_type=jnp.float32)

    def product(buf, rows, chosen):
        def body(k, carry):
            pl.when(chosen(k))(lambda: add_product(buf, rows, k))
            return carry

        lax.fori_loop(first, stop, body, 0)

    def far_product(buf, rows):
        pl.when((far_k >= first) & (far_k < stop))(lambda: add_product(buf, rows, far_k))

    far_k = jnp.where(far > zh, plane - 4 + far, plane + 4 + far)

    def early(k):
        return ((k >= plane) & (k < plane + 4)) | (k == r - 4) | (k == r + 4)

    def early_both(k):
        return early(k) & (k != c + 3 * f) & (k != c - 3 * f)

    def middle(chosen):
        return lambda k: jnp.logical_not(chosen(k) | (k == far_k))

    def square_piece(a):
        rows = pl.ds(a * BLOCK, BLOCK)
        far_product(right, rows)
        value = acc[rows, :] * mask_ref[pl.ds(a, 1), mine]
        square_ref[rows, :] = value
        cube[own_right, rows, :] = value.astype(jnp.bfloat16)
        acc[rows, :] = jnp.zeros((BLOCK, width), jnp.float32)

    gather(right, right_recv, True, own_piece)
    acc[...] = jnp.zeros_like(acc)

    def from_sibling(names):
        for name in names:
            for j in ((0, 1) if name != "RF" else (0,)) if name != "G" else (1,):
                arrived(left.at[left_slot[name], 1 - l, halves[j]], sib_recv.at[left_slot[name], j])

    from_sibling(("A1", "YF", "YN", "PF", "TF", "TN"))
    own_arrived(right, right_recv)
    for rows in halves:
        product(right, rows, early_both)
    from_sibling(("PN", "RF", "G"))
    near_arrived(right, right_recv)
    for rows in halves:
        product(right, rows, middle(early_both))
    far_arrived(right, right_recv)

    started = len(sent)
    gather(cube, cube_recv, False, square_piece)
    square_copy = pltpu.make_async_copy(square_ref, square_hbm, local_sems.at[0])
    square_copy.start()
    left_device(sent[:started])
    own_arrived(cube, cube_recv)
    for rows in halves:
        product(cube, rows, early)
    near_arrived(cube, cube_recv)
    for rows in halves:
        product(cube, rows, middle(early))
    left_device(sent[started:])
    far_arrived(cube, cube_recv)
    sign_copies = []
    for j, rows in enumerate(halves):
        far_product(cube, rows)
        for a in range(j * count // 2, (j + 1) * count // 2):
            block = pl.ds(a * BLOCK, BLOCK)
            row_mask = mask_ref[pl.ds(a, 1), mine]
            sparse = mat_ref[block, mine] * row_mask
            sign_ref[block, :] = row_mask * (1.5 * sparse - 0.5 * acc[block, :])
        sign_copies.append(pltpu.make_async_copy(sign_ref.at[rows], sign_hbm.at[rows], local_sems.at[1 + j]))
        sign_copies[-1].start()

    square_copy.wait()
    for copy in sign_copies:
        copy.wait()


def per_device(matrix, band_cols):
    tile = matrix.shape[0]
    width = tile // 2
    piece = tile // PIECES
    out = jax.ShapeDtypeStruct((tile, width), jnp.float32)
    return pl.pallas_call(
        kernel,
        out_shape=(out, out),
        in_specs=[pl.BlockSpec(memory_space=pltpu.HBM)] * 2,
        out_specs=(pl.BlockSpec(memory_space=pltpu.HBM),) * 2,
        scratch_shapes=[
            pltpu.VMEM((10, 2, tile, width), jnp.bfloat16),
            pltpu.VMEM((14, tile, width), jnp.bfloat16),
            pltpu.VMEM((14, tile, width), jnp.bfloat16),
            pltpu.VMEM((2, 3 * PIECES, piece, width), jnp.bfloat16),
            pltpu.VMEM((8, tile), jnp.float32),
            pltpu.VMEM((tile, width), jnp.float32),
            pltpu.VMEM((tile, tile), jnp.float32),
            pltpu.VMEM((tile, width), jnp.float32),
            pltpu.VMEM((tile, width), jnp.float32),
            pltpu.SMEM(band_cols.shape[::-1], jnp.int32),
            pltpu.SemaphoreType.DMA((10, PIECES)),
            pltpu.SemaphoreType.DMA((10, 2)),
            pltpu.SemaphoreType.DMA((14, PIECES)),
            pltpu.SemaphoreType.DMA((14, PIECES)),
            pltpu.SemaphoreType.DMA((2, 3 * PIECES)),
            pltpu.SemaphoreType.DMA((128,)),
            pltpu.SemaphoreType.DMA((1 + PIECES,)),
        ],
        compiler_params=pltpu.CompilerParams(
            collective_id=0, has_side_effects=True, vmem_limit_bytes=105 * 2**19),
        cost_estimate=pl.CostEstimate(flops=4 * 10**9, bytes_accessed=2 * 2**20, transcendentals=0),
    )(band_cols.T, matrix)


def solution(mesh):
    in_specs = (P("row", "col"), P())
    out_specs = (P("row", ("col", "layer")), P("row", ("col", "layer")))
    return jax.shard_map(
        per_device, mesh=mesh, in_specs=in_specs, out_specs=out_specs, check_vma=False
    )
```

```python
import jax
import jax.numpy as jnp
from jax import lax
from jax.experimental import pallas as pl
from jax.experimental.pallas import tpu as pltpu
from jax.sharding import PartitionSpec as P

BLOCK = 128
REACH = 4
PIECES = 4
MESH = pl.DeviceIdType.MESH
NEEDS = {"A2": "A1", "B2": "B1", "A3": "A2", "B3": "B2", "A4": "A3", "B4": "B3", "XA": "A2", "XB": "B2", "KA": "XA", "KB": "XB",
         "LA": "KA", "LB": "KB", "FA": "A4", "FB": "B4", "TF": "YF", "TN": "YN", "PF": "A1", "PN": "A1", "RF": "PF", "G": "TN"}
LINKS = {"A1": "zp", "B1": "zo", "A2": "zo", "B2": "zp", "A3": "zp", "B3": "zo", "A4": "zo", "B4": "zp", "YF": "yf", "YN": "yn",
         "TF": "yf", "TN": "yn", "PF": "yf", "PN": "yn", "RF": "yf", "G": "zp"}
REVERSED = ("B1", "B2", "B3", "B4", "XB", "KB", "LB", "FB")
ROWS = ("YF", "YN", "TF", "TN", "PF", "PN", "RF", "G")
COARSE = ROWS + ("XS",)
SQUARE_ORDER = (
    "A10", "B13", "YF0", "A11", "B11", "YF1", "XO0", "B10", "A13", "XO3", "YN1", "A20", "A12", "YN0",
    "B12", "B21", "A21", "XS1", "TF0", "XO2", "B20", "PF0", "B23", "TN1", "XO1", "A22", "XA0", "A23",
    "A30", "XB1", "PN0", "B31", "TF1", "XA1", "A31", "XB0", "PF1", "B30", "PN1", "B22", "XB3", "XS0",
    "XA2", "KA0", "A40", "XA3", "A41", "B41", "TN0", "?TF0", "RF0", "KB0", "XB2", "B40", "G1", "?TF1",
    "FA0", "?PN1", "FA1", "LA0", "?PF0", "FB1", "?TN0", "LB0", "?PF1", "?TN1", "FB0", "?G1", "?RF0", "?PN0",
)
CUBE_ORDER = (
    "A10", "B10", "XO0", "XS0", "A11", "B11", "XO1", "A12", "B12", "XO2", "XS1", "A13", "A20", "XO3",
    "A21", "B20", "B13", "B21", "XA0", "A22", "B22", "XA1", "XB0", "A30", "B30", "XB1", "B23", "B31",
    "KA0", "XB2", "A23", "A31", "KB0", "XA2", "A40", "B40", "XB3", "B41", "LA0", "A41", "XA3", "LB0",
    "FB0", "FB1", "FA0", "FA1",
)


def kernel(band_hbm, mat_hbm, sign_hbm, square_hbm, left, right, cube, relay, mask_ref, acc, mat_ref, square_ref, sign_ref, band_ref,
           left_recv, sib_recv, right_recv, cube_recv, relay_recv, send_sems, local_sems):
    r = lax.axis_index("row")
    c = lax.axis_index("col")
    l = lax.axis_index("layer")
    tile = mat_hbm.shape[0]
    width = tile // 2
    count = tile // BLOCK
    piece = tile // PIECES
    x, zh = r // 4, r % 4
    y, zl = c // 2, c % 2
    ol = 1 - zl
    f = 1 - 2 * zl
    order = (0, 3, 1, 2)

    band_copy = pltpu.make_async_copy(band_hbm, band_ref, local_sems.at[0])
    band_copy.start()
    mat_copies = {}
    for p in order:
        rows = pl.ds(p * piece, piece)
        mat_copies[p] = pltpu.make_async_copy(mat_hbm.at[rows], mat_ref.at[rows], local_sems.at[1 + p])
        mat_copies[p].start()

    def at(dx=0, dzh=0, dy=0, zlow=zl):
        return (((x + dx + 4) % 4) * 4 + (zh + dzh + 4) % 4, ((y + dy + 8) % 8) * 2 + zlow, l)

    sibling = (r, c, 1 - l)
    xup, xdown = at(dx=1), at(dx=-1)
    device = {"zp": at(zlow=ol), "zo": at(dzh=-f, zlow=ol), "x": xup, "w": xdown, "yf": at(dy=f), "yn": at(dy=-f)}

    barrier = pltpu.get_barrier_semaphore()
    for other in (sibling, *device.values()):
        pl.semaphore_signal(barrier, inc=1, device_id=other, device_id_type=MESH)

    column = 4 * c + lax.broadcasted_iota(jnp.int32, (1, tile), 1) // BLOCK
    own_left = 4 + zl
    own_right = 4 + zh
    mine = pl.ds(pl.multiple_of(l * width, width), width)
    band_copy.wait()

    def own_piece(a):
        hit = column == band_ref[0, count * r + a]
        for j in range(1, band_ref.shape[0]):
            hit = hit | (column == band_ref[j, count * r + a])
        row_mask = jnp.where(hit, 1.0, 0.0).astype(jnp.float32)
        mask_ref[pl.ds(a, 1), :] = row_mask
        rows = pl.ds(a * BLOCK, BLOCK)
        mat_copies[a].wait()
        low = (mat_ref[rows, :] * row_mask).astype(jnp.bfloat16)
        left[own_left, 0, rows, :] = low[:, :width]
        left[own_left, 1, rows, :] = low[:, width:]
        right[own_right, rows, :] = left[own_left, l, rows, :]

    sent = []

    def remote(src, dst, recv_sem, target):
        return pltpu.make_async_remote_copy(
            src_ref=src, dst_ref=dst, send_sem=send_sems.at[len(sent)], recv_sem=recv_sem,
            device_id=target, device_id_type=MESH)

    def send(src, dst, recv_sem, target):
        copy = remote(src, dst, recv_sem, target)
        copy.start()
        sent.append((copy, None))

    def left_device(copies):
        for copy, only in copies:
            if only is None:
                copy.wait_send()
            else:
                pl.when(only)(copy.wait_send)

    def arrival(ref, sem):
        return pltpu.make_async_remote_copy(
            src_ref=ref, dst_ref=ref, send_sem=send_sems.at[0], recv_sem=sem,
            device_id=sibling, device_id_type=MESH)

    def arrived(ref, sem):
        arrival(ref, sem).wait_recv()

    left_slot = {"YF": 4 - 2 * f + zl, "YN": 4 + 2 * f + zl, "TF": 4 - 4 * f + zl, "TN": 4 + 4 * f + zl,
                 "PF": 4 - 2 * f + ol, "PN": 4 + 2 * f + ol, "RF": 4 - 4 * f + ol, "G": 4 - 4 * f + ol, "A1": 4 + ol}
    near_a, near_b, far = (zh - f + 4) % 4, (zh + f + 4) % 4, (zh + 2) % 4
    halves = [pl.ds(j * width, width) for j in range(2)]
    edge = (zh == 0) | (zh == 3)
    side = (jnp.where(zh < 2, xdown[0], xup[0]), c, l)

    def gather(buf, sem, square, make_piece):
        phase = 0 if square else 1
        waited, made = set(), set()

        def rows_of(name, i):
            if name in COARSE:
                return halves[i]
            p = PIECES - 1 - i if name in REVERSED else i
            return pl.ds(p * piece, piece)

        def ensure(name, i):
            for p in ((2 * i, 2 * i + 1) if name in COARSE else (PIECES - 1 - i if name in REVERSED else i,)):
                if p not in made:
                    made.add(p)
                    make_piece(p)
                    if len(made) == 1 and square:
                        pl.semaphore_wait(barrier, 1 + len(device))

        def landing(name, i):
            if name in left_slot and (square or name != "A1"):
                slot = left_slot[name]
                return left.at[slot, l, rows_of(name, i)], left_recv.at[slot, i]
            if name in ("XA", "XB", "KA", "KB"):
                slot = 12 if name in ("XA", "XB") else 13
                return buf.at[slot, rows_of(name, i)], sem.at[slot, 0 if name in ("XA", "KA") else 1]
            if name in ("A1", "B1", "A3", "B3"):
                place = {"A1": 0, "B1": PIECES, "A3": 2 * PIECES, "B3": 2 * PIECES + 2}[name] + i
                return relay.at[phase, place], relay_recv.at[phase, place]
            slot = 4 + {"A2": near_a, "B2": near_b, "A4": far, "B4": far}[name]
            return buf.at[slot, rows_of(name, i)], sem.at[slot, i + (2 if name == "B4" else 0)]

        def wait(name, i):
            if (name, i) in waited:
                return
            waited.add((name, i))
            arrived(*landing(name, i))
            if name in left_slot and square:
                if name == "A1":
                    if (name, i ^ 1) not in waited:
                        return
                    i = i // 2
                ref = left.at[left_slot[name], l, halves[i]]
                send(ref, ref, sib_recv.at[left_slot[name], i], sibling)

        def away(name, i):
            if name in ("XO", "XS", "XA", "XB", "LA", "LB", "FA", "FB"):
                zs = {"A": near_a, "B": near_b}.get(name[1], zh) if name[0] != "F" else far
                higher = {"XO": zh < 2, "XS": zh >= 2}.get(name, zs > zh)
                slot = jnp.where(higher, zs, 8 + zs)
                target = jnp.where(higher, xup[0], xdown[0])
                index = i + (2 if name == "FB" else 0)
                if name in ("LA", "LB"):
                    target = side[0]
                if name in ("XA", "XB") and i == 0:
                    slot = jnp.where(edge, 12, slot)
                    target = jnp.where(edge, side[0], target)
                    index = jnp.where(edge, 0 if name == "XA" else 1, 0)
                return buf.at[slot, rows_of(name, i)], sem.at[slot, index], (target, c, l)
            if name in ("KA", "KB"):
                return *landing(name, i), side
            target = device[LINKS[name]]
            if name == "A1" and square:
                return left.at[own_left, l, rows_of(name, i)], left_recv.at[own_left, i], target
            if name == "G":
                slot = left_slot["TN"]
                return left.at[slot, l, halves[i]], left_recv.at[slot, i], target
            if name in ("A1", "B1", "A3", "B3") or name in ROWS:
                return *landing(name, i), target
            slot = 4 + {"A2": zh, "B2": near_a, "A4": near_b, "B4": far}[name]
            return buf.at[slot, rows_of(name, i)], sem.at[slot, i + (2 if name == "B4" else 0)], target

        for token in SQUARE_ORDER if square else CUBE_ORDER:
            name, i = token[:-1].lstrip("?"), int(token[-1])
            needs = [(NEEDS[name], i)] if NEEDS.get(name) else []
            if name in ("PF", "PN"):
                needs = [("A1", 2 * i), ("A1", 2 * i + 1)]
            if token[0] == "?":
                wait(name, i)
            elif name in ("KA", "KB", "LA", "LB"):
                source, recv = landing(*needs[0])
                before = arrival(source, recv)
                copy = remote(source, *away(name, i))
                sent.append((copy, edge))

                @pl.when(edge)
                def _():
                    before.wait_recv()
                    copy.start()
            else:
                for m in needs:
                    wait(*m)
                if name in ROWS and needs:
                    source = left.at[left_slot[needs[0][0]], l, halves[i]]
                elif needs:
                    source = landing(*needs[0])[0]
                else:
                    ensure(name, i)
                    source = left.at[own_left, l, halves[i]] if name in ROWS else buf.at[own_right, rows_of(name, i)]
                send(source, *away(name, i))

    def own_arrived(buf, sem):
        for i in range(PIECES):
            slot = jnp.where(zh < 2, zh, 8 + zh)
            arrived(buf.at[slot, pl.ds(i * piece, piece)], sem.at[slot, i])
        for i in range(2):
            slot = jnp.where(zh < 2, 8 + zh, zh)
            arrived(buf.at[slot, halves[i]], sem.at[slot, i])

    def near_arrived(buf, sem):
        for i in range(PIECES):
            for p, zs in ((i, near_a), (PIECES - 1 - i, near_b)):
                slot = jnp.where(zs > zh, zs, 8 + zs)
                arrived(buf.at[slot, pl.ds(p * piece, piece)], sem.at[slot, i])

    def far_arrived(buf, sem):
        slot = jnp.where(far > zh, far, 8 + far)
        for i in range(2):
            arrived(buf.at[slot, pl.ds(i * piece, piece)], sem.at[slot, i])
            arrived(buf.at[slot, pl.ds((PIECES - 1 - i) * piece, piece)], sem.at[slot, i + 2])

    first = jnp.maximum(jnp.maximum(r, c) - REACH, 0)
    stop = jnp.minimum(jnp.minimum(r, c) + REACH, 15) + 1
    inside = (c - r <= REACH) & (r - c <= REACH)
    stop = jnp.where(inside, stop, first)
    plane = 4 * x

    def add_product(buf, rows, k):
        ls = k - c + zl + 4
        rs = k - r + zh + 4
        acc[rows, :] += jnp.dot(
            left[ls, 0, rows, :], buf[rs, :width, :], preferred_element_type=jnp.float32) + jnp.dot(
            left[ls, 1, rows, :], buf[rs, width:, :], preferred_element_type=jnp.float32)

    def product(buf, rows, chosen):
        def body(k, carry):
            pl.when(chosen(k))(lambda: add_product(buf, rows, k))
            return carry

        lax.fori_loop(first, stop, body, 0)

    def far_product(buf, rows):
        pl.when((far_k >= first) & (far_k < stop))(lambda: add_product(buf, rows, far_k))

    far_k = jnp.where(far > zh, plane - 4 + far, plane + 4 + far)

    def early(k):
        return ((k >= plane) & (k < plane + 4)) | (k == r - 4) | (k == r + 4)

    def early_both(k):
        return early(k) & (k != c + 3 * f) & (k != c - 3 * f)

    def middle(chosen):
        return lambda k: jnp.logical_not(chosen(k) | (k == far_k))

    def square_piece(a):
        rows = pl.ds(a * BLOCK, BLOCK)
        far_product(right, rows)
        cube[own_right, rows, :] = (acc[rows, :] * mask_ref[pl.ds(a, 1), mine]).astype(jnp.bfloat16)

    gather(right, right_recv, True, own_piece)
    acc[...] = jnp.zeros_like(acc)

    def from_sibling(names):
        for name in names:
            for j in ((0, 1) if name != "RF" else (0,)) if name != "G" else (1,):
                arrived(left.at[left_slot[name], 1 - l, halves[j]], sib_recv.at[left_slot[name], j])

    from_sibling(("A1", "YF", "YN", "PF", "TF", "TN"))
    own_arrived(right, right_recv)
    for rows in halves:
        product(right, rows, early_both)
    from_sibling(("PN", "RF", "G"))
    near_arrived(right, right_recv)
    for rows in halves:
        product(right, rows, middle(early_both))
    far_arrived(right, right_recv)

    started = len(sent)
    gather(cube, cube_recv, False, square_piece)
    for a in range(count):
        rows = pl.ds(a * BLOCK, BLOCK)
        square_ref[rows, :] = acc[rows, :] * mask_ref[pl.ds(a, 1), mine]
        acc[rows, :] = jnp.zeros((BLOCK, width), jnp.float32)
    square_copy = pltpu.make_async_copy(square_ref, square_hbm, local_sems.at[0])
    square_copy.start()
    left_device(sent[:started])
    own_arrived(cube, cube_recv)
    for rows in halves:
        product(cube, rows, early)
    near_arrived(cube, cube_recv)
    for rows in halves:
        product(cube, rows, middle(early))
    left_device(sent[started:])
    far_arrived(cube, cube_recv)
    sign_copies = []
    for j, rows in enumerate(halves):
        far_product(cube, rows)
        for a in range(j * count // 2, (j + 1) * count // 2):
            block = pl.ds(a * BLOCK, BLOCK)
            row_mask = mask_ref[pl.ds(a, 1), mine]
            sparse = mat_ref[block, mine] * row_mask
            sign_ref[block, :] = row_mask * (1.5 * sparse - 0.5 * acc[block, :])
        sign_copies.append(pltpu.make_async_copy(sign_ref.at[rows], sign_hbm.at[rows], local_sems.at[1 + j]))
        sign_copies[-1].start()

    square_copy.wait()
    for copy in sign_copies:
        copy.wait()


def per_device(matrix, band_cols):
    tile = matrix.shape[0]
    width = tile // 2
    piece = tile // PIECES
    out = jax.ShapeDtypeStruct((tile, width), jnp.float32)
    return pl.pallas_call(
        kernel,
        out_shape=(out, out),
        in_specs=[pl.BlockSpec(memory_space=pltpu.HBM)] * 2,
        out_specs=(pl.BlockSpec(memory_space=pltpu.HBM),) * 2,
        scratch_shapes=[
            pltpu.VMEM((10, 2, tile, width), jnp.bfloat16),
            pltpu.VMEM((14, tile, width), jnp.bfloat16),
            pltpu.VMEM((14, tile, width), jnp.bfloat16),
            pltpu.VMEM((2, 3 * PIECES, piece, width), jnp.bfloat16),
            pltpu.VMEM((8, tile), jnp.float32),
            pltpu.VMEM((tile, width), jnp.float32),
            pltpu.VMEM((tile, tile), jnp.float32),
            pltpu.VMEM((tile, width), jnp.float32),
            pltpu.VMEM((tile, width), jnp.float32),
            pltpu.SMEM(band_cols.shape[::-1], jnp.int32),
            pltpu.SemaphoreType.DMA((10, PIECES)),
            pltpu.SemaphoreType.DMA((10, 2)),
            pltpu.SemaphoreType.DMA((14, PIECES)),
            pltpu.SemaphoreType.DMA((14, PIECES)),
            pltpu.SemaphoreType.DMA((2, 3 * PIECES)),
            pltpu.SemaphoreType.DMA((128,)),
            pltpu.SemaphoreType.DMA((1 + PIECES,)),
        ],
        compiler_params=pltpu.CompilerParams(
            collective_id=0, has_side_effects=True, vmem_limit_bytes=105 * 2**19),
        cost_estimate=pl.CostEstimate(flops=4 * 10**9, bytes_accessed=2 * 2**20, transcendentals=0),
    )(band_cols.T, matrix)


def solution(mesh):
    in_specs = (P("row", "col"), P())
    out_specs = (P("row", ("col", "layer")), P("row", ("col", "layer")))
    return jax.shard_map(
        per_device, mesh=mesh, in_specs=in_specs, out_specs=out_specs, check_vma=False
    )
```
